32 devices in a mesh: seq: 4 (over y, x), exp: 8 (over z, core).
Axes of the slice: x: 2, y: 2, z: 4, core: 2. Of those that a mesh axis runs over, the one named last changes fastest.
Arguments:
- queries: bfloat16 [128, 64, 576], P(('seq', 'exp')), may hold values from -68 to 68
- own_latent: bfloat16 [128, 576], P(('seq', 'exp')), may hold values from -4 to 4
- snapshots: bfloat16 [2, 2048, 576], P(None, 'seq'), may hold values from -12 to 12
- leaf_snapshot: int32 [128], P(('seq', 'exp')), may hold values from 0 to 1
- moe_input: bfloat16 [128, 7168], P(('seq', 'exp')), may hold values from -6 to 6
- expert_ids: int32 [128, 8], P(('seq', 'exp')), may hold values from 0 to 7, all different within a row; in each aligned block of 4 rows (0 to 3, 4 to 7, ...) at most 4 rows name the same one
- gate_weights: float32 [128, 8], P(('seq', 'exp')), may hold values from 0.05 to 0.5
- w_gate: bfloat16 [8, 7168, 2048], P('exp', None, 'seq'), may hold values from -0.0625 to 0.0625
- w_up: bfloat16 [8, 7168, 2048], P('exp', None, 'seq'), may hold values from -0.0625 to 0.0625
- w_down: bfloat16 [8, 2048, 7168], P('exp', 'seq'), may hold values from -0.125 to 0.125
Outputs:
- attn_latent: bfloat16 [128, 64, 512], P(('seq', 'exp'))
- moe_output: bfloat16 [128, 7168], P(('seq', 'exp'))
The draws below stay inside these ranges and needn't reach their ends.
Inputs may be any that keep to these rules, and one draw needn't show every extreme that they name: `expert_ids`: each row names 8 different experts; among the 4 rows of one device, no expert is named more than 4 times.
All inputs are finite; a program needn't handle non-finite values.
Results may differ from the reference program's by a relative error of at most 0.02.
Values may be sent and summed in bfloat16 or wider, within the bound.
A program may use at most 192 MiB of HBM per device.

```python
import math
import jax
import jax.numpy as jnp
import numpy as np
from jax import lax

D = 7168
FF = 2048
LAT = 512
TOP = 8
HEADS = 64
KDIM = 576
FF_DEV = 512
EXPERTS = 8
LEAF_DEV = 4
CAP = 4
POS_DEV = 512
SNAPS = 2
SNAP_LEN = 2048
LEAVES = 128


qk_scale = 192.0 ** (-0.5)


def own_values(key, rope_factor):
    base = jax.random.truncated_normal(jax.random.fold_in(key, 7), -4.0, 4.0, (LEAVES, KDIM), jnp.float32)
    factor = jnp.where(jnp.arange(KDIM) < LAT, 1.0, rope_factor)
    return base * factor[None, :]


def own_share():
    return (math.log(SNAP_LEN) + 1.0) / (qk_scale * KDIM)


def draw_own_latent(key, part):
    values = own_values(key, 1.0)
    return values.astype(jnp.bfloat16)


def draw_queries(key, part):
    noise = jax.random.truncated_normal(jax.random.fold_in(key, 13), -4.0, 4.0, (LEAVES, HEADS, KDIM), jnp.float32)
    mixed = 0.5 * noise + own_share() * own_values(key, 1.0)[:, None, :]
    return mixed.astype(jnp.bfloat16)


def draw_snapshots(key, part):
    log_scale = jax.random.uniform(jax.random.fold_in(key, 17), (SNAPS, SNAP_LEN, 1), jnp.float32, math.log(0.5), math.log(3.0))
    row_scale = jnp.exp(log_scale)
    values = jax.random.truncated_normal(jax.random.fold_in(key, 19), -4.0, 4.0, (SNAPS, SNAP_LEN, KDIM), jnp.float32)
    values = values * row_scale
    return values.astype(jnp.bfloat16)


def touch_ends(result, stream_key, least, high):
    place = [jax.random.randint(jax.random.fold_in(stream_key, axis), (), 0, length) for axis, length in enumerate(result.shape)]
    main_axis = result.shape.index(max(result.shape))
    beside = place[:main_axis] + [(place[main_axis] + 1) % result.shape[main_axis]] + place[main_axis + 1:]
    return result.at[tuple(place)].set(least).at[tuple(beside)].set(high)


def levels(key, shape, split, least, top_value):
    def one(dim, shards_of):
        heights = jax.random.uniform(jax.random.fold_in(jax.random.fold_in(key, 6), dim), (shards_of,), jnp.float32, least / len(split), top_value / len(split))
        return jnp.repeat(jnp.exp(heights), shape[dim] // shards_of).reshape((-1,) + (1,) * (len(shape) - dim - 1))

    gain = one(*split[0])
    for cut in split[1:]:
        gain = gain * one(*cut)
    return gain


def routed_block(key, own, number, rows, count, top, reach, slope):
    sequence = jax.random.permutation(key, count)
    crowded, usual = shares(count, rows * top, reach, slope, True), shares(count, rows * top, reach, slope, False)
    places = jnp.arange(count)

    def named(tallies, offset_by):
        used = int((tallies > 0).sum())
        fixed = max(1, used // 4)
        shifted = fixed + (places - fixed + offset_by * (used - fixed)) % max(1, count - fixed)
        return jnp.zeros((count,), jnp.int32).at[sequence[jnp.where(places < fixed, places, shifted)]].set(jnp.asarray(tallies, jnp.int32))

    tallies = jnp.where(number % 4 == 0, named(crowded, number // 4), named(usual, number - number // 4 - 1))
    mixed = jax.random.permutation(jax.random.fold_in(own, 3), count)
    donor, receiver = mixed[0:count // 2 * 2:2], mixed[1:count // 2 * 2:2]
    slack = jnp.minimum(tallies[donor] - 1, reach - tallies[receiver]) // 2
    slack = jnp.where((donor == sequence[0]) | (receiver == sequence[0]) | (tallies[receiver] == 0), 0, jnp.maximum(slack, 0))
    shifted = jax.random.randint(jax.random.fold_in(own, 4), (count // 2,), 0, 1 << 20) % (slack + 1)
    tallies = tallies.at[donor].add(-shifted).at[receiver].add(shifted)
    items = jnp.searchsorted(jnp.cumsum(tallies), jnp.arange(rows * top), side="right").astype(jnp.int32)
    grid = items.reshape(top, rows).T
    grid = grid[jax.random.permutation(jax.random.fold_in(own, 1), rows)]
    offset_by = jax.random.randint(jax.random.fold_in(own, 2), (rows, 1), 0, top)
    return jnp.take_along_axis(grid, (jnp.arange(top)[None, :] + offset_by) % top, axis=1)


def shares(count, total, limit, lean, full):
    portions = [(1 << 20) // math.isqrt(standing ** lean) + 1 for standing in range(1, count + 1)]
    largest = limit if full else min(limit, max(-(-total // count), total * portions[0] // sum(portions)))
    least = 1 if total - largest >= count - 1 else 0
    counts, rest = [largest] + [least] * (count - 1), total - largest - least * (count - 1)
    while rest > 0:
        movable = [i for i in range(1, count) if counts[i] < largest] or [i for i in range(1, count) if counts[i] < limit]
        mass, left = sum([portions[i] for i in movable]), rest
        for i in movable:
            extra = min(limit - counts[i], max(1, left * portions[i] // mass), rest)
            counts[i] = counts[i] + extra
            rest = rest - extra
    return np.array(counts)


def scatter_about(key, extent, scale, bound, shards=(), held_as=jnp.bfloat16):
    result = jax.random.normal(key, extent, jnp.float32) * scale
    if len(shards) > 0:
        result = levels(key, extent, shards, -0.22, 0.18) * result
    return jnp.clip(result, min=-bound, max=bound).astype(held_as)


def setup_inputs(seed: int = 0) -> dict:
    splits = jax.random.split(jax.random.key(seed), 11)
    queries = draw_queries(jax.random.fold_in(splits[10], 71), 0)
    own_latent = draw_own_latent(jax.random.fold_in(splits[10], 71), 0)
    snapshots = draw_snapshots(jax.random.fold_in(splits[10], 71), 0)
    leaf_snapshot = touch_ends(jax.random.randint(splits[3], (LEAVES,), 0, SNAPS), jax.random.fold_in(splits[3], 1), 0, SNAPS - 1).astype(jnp.int32)
    moe_input = scatter_about(splits[4], (LEAVES, D), 1.0, 6.0, ((0, 32),))
    expert_ids_keys = jax.random.split(jax.random.fold_in(splits[5], 1), LEAVES // LEAF_DEV)
    expert_ids_turns = jax.random.permutation(jax.random.fold_in(splits[5], 3), LEAVES // LEAF_DEV)
    expert_ids = jax.vmap(lambda own, number: routed_block(jax.random.fold_in(splits[5], 2), own, number, LEAF_DEV, EXPERTS, TOP, CAP, 2))(expert_ids_keys, expert_ids_turns).reshape((LEAVES, TOP))
    gate_weights = jnp.clip(jnp.exp(math.log(0.5) - 2.3025851 * jax.random.uniform(splits[6], (LEAVES, TOP), jnp.float32) ** levels(splits[6], (LEAVES, TOP), ((0, 32),), -0.2, 0.2)), 0.05, 0.5)
    w_gate = scatter_about(splits[7], (EXPERTS, D, FF), D ** -0.5, 0.0625, ((0, 8), (2, 4)))
    w_up = scatter_about(splits[8], (EXPERTS, D, FF), D ** -0.5, 0.0625, ((0, 8), (2, 4)))
    w_down = scatter_about(splits[9], (EXPERTS, FF, D), FF ** -0.5, 0.125, ((0, 8), (1, 4)))
    return dict(queries=queries, own_latent=own_latent, snapshots=snapshots, leaf_snapshot=leaf_snapshot, moe_input=moe_input, expert_ids=expert_ids, gate_weights=gate_weights, w_gate=w_gate, w_up=w_up, w_down=w_down)


qk_scale = 192.0 ** -0.5


def attend_leaf(query_heads, snapshot_rows, own_key):
    scores = qk_scale * jnp.dot(query_heads, snapshot_rows.T, preferred_element_type=jnp.float32)
    own_score = qk_scale * jnp.dot(query_heads, own_key, preferred_element_type=jnp.float32)
    row_max = jnp.maximum(jnp.max(scores, axis=1), own_score)
    weights = jnp.exp(scores - row_max[:, None]).astype(jnp.bfloat16)
    block_count = SNAP_LEN // POS_DEV
    blocked = weights.reshape(HEADS, block_count, POS_DEV).astype(jnp.float32)
    mass_parts = jnp.sum(blocked, axis=2)
    mass_parts = lax.optimization_barrier(mass_parts.astype(jnp.bfloat16)).astype(jnp.float32)
    latent_blocks = snapshot_rows[:, :LAT].reshape(block_count, POS_DEV, LAT).astype(jnp.float32)
    value_parts = jnp.einsum("hbp,bpl->hbl", blocked, latent_blocks, precision=lax.Precision.HIGHEST)
    value_parts = lax.optimization_barrier(value_parts.astype(jnp.bfloat16)).astype(jnp.float32)
    own_weight = jnp.exp(own_score - row_max)
    numerator = jnp.sum(value_parts, axis=1) + own_weight[:, None] * own_key[:LAT].astype(jnp.float32)
    denominator = jnp.sum(mass_parts, axis=1) + own_weight
    return (numerator / denominator[:, None]).astype(jnp.bfloat16)


def attention(queries, own_latent, snapshots, leaf_snapshot):
    def one_leaf(packed):
        query_heads, own_key, snapshot_index = packed
        snapshot_rows = lax.dynamic_index_in_dim(snapshots, snapshot_index, 0, keepdims=False)
        return attend_leaf(query_heads, snapshot_rows, own_key)

    return lax.map(one_leaf, (queries, own_latent, leaf_snapshot))


def expert_block(packed):
    slot_rows, gate_matrix, up_matrix, down_matrix = packed
    flat_rows = slot_rows.reshape(-1, D)
    gate_proj = jnp.dot(flat_rows, gate_matrix, preferred_element_type=jnp.float32)
    up_proj = jnp.dot(flat_rows, up_matrix, preferred_element_type=jnp.float32)
    hidden = (jax.nn.silu(gate_proj) * up_proj).astype(jnp.bfloat16)
    summed = jnp.zeros((flat_rows.shape[0], D), jnp.float32)
    for slice_index in range(FF // FF_DEV):
        offset = slice_index * FF_DEV
        partial_out = jnp.dot(hidden[:, offset:offset + FF_DEV], down_matrix[offset:offset + FF_DEV], preferred_element_type=jnp.float32)
        summed = summed + lax.optimization_barrier(partial_out.astype(jnp.bfloat16)).astype(jnp.float32)
    return summed.astype(jnp.bfloat16).reshape(slot_rows.shape)


def mixture(moe_input, expert_ids, gate_weights, w_gate, w_up, w_down):
    source_count = LEAVES // LEAF_DEV
    ids_blocked = expert_ids.reshape(source_count, LEAF_DEV, TOP)
    chosen = (ids_blocked[..., None] == jnp.arange(EXPERTS, dtype=jnp.int32)).astype(jnp.int32)
    per_row = jnp.sum(chosen, axis=2).astype(jnp.int32)
    earlier = (jnp.cumsum(per_row, axis=1) - per_row).astype(jnp.int32)
    slot_rank = jnp.take_along_axis(earlier, ids_blocked, axis=2).astype(jnp.int32)
    source_index = jnp.broadcast_to(jnp.arange(source_count, dtype=jnp.int32)[:, None, None], ids_blocked.shape)
    inputs_blocked = jnp.broadcast_to(moe_input.reshape(source_count, LEAF_DEV, 1, D), (source_count, LEAF_DEV, TOP, D))
    slot_table = jnp.zeros((EXPERTS, source_count, CAP, D), jnp.bfloat16)
    slot_table = slot_table.at[ids_blocked, source_index, slot_rank].set(inputs_blocked)
    outputs = lax.map(expert_block, (slot_table, w_gate, w_up, w_down))
    picked = outputs[ids_blocked, source_index, slot_rank]
    weighted = jnp.sum(gate_weights.reshape(source_count, LEAF_DEV, TOP, 1) * picked.astype(jnp.float32), axis=2)
    return weighted.reshape(LEAVES, D).astype(jnp.bfloat16)


def reference(queries, own_latent, snapshots, leaf_snapshot, moe_input, expert_ids, gate_weights, w_gate, w_up, w_down):
    attn_latent = attention(queries, own_latent, snapshots, leaf_snapshot)
    moe_output = mixture(moe_input, expert_ids, gate_weights, w_gate, w_up, w_down)
    return (attn_latent, moe_output)
```

```python
import functools

import jax
import jax.numpy as jnp
from jax import lax
from jax.experimental import pallas as pl
from jax.experimental.pallas import tpu as pltpu
from jax.sharding import PartitionSpec as P

LAT = 512
LANES = 128
CHUNKS = 2
CORES = 2
MESH = pl.DeviceIdType.MESH

qk_scale = 192.0 ** (-0.5)


def kernel(
    ns, ne, q, own, snap_hbm, leaf, x, ids, gw, wg, wu, wd, attn_out, moe_out,
    wg_v, wu_v, wd_v, snap, zbuf, asm, xs, hid, pbuf, r1, r2s, r2r, r3s, r3r, m_s, l_s, acc,
    w_sem, sl_sem, a1_s, a1_r, a2_s, a2_r, a3_s, a3_r, sn_s, sn_r, sf_s, sf_r,
    b1_s, b1_r, b2_s, b2_r, b3_s, b3_r,
):
    rows, width = x.shape
    nz = ne // CORES
    heads = q.shape[0] // rows
    cw = width // CHUNKS
    s, e = lax.axis_index("seq"), lax.axis_index("exp")
    z, c = e // CORES, e % CORES
    sib = (s, z * CORES + (1 - c))

    def zpeer(k):
        return lax.rem(z + k, nz)

    def speer(k):
        return lax.rem(s + k, ns)

    def sfrom(k):
        return lax.rem(s + ns - k, ns)

    def remote(src, dst, send, recv, device):
        return pltpu.make_async_remote_copy(
            src_ref=src, dst_ref=dst, send_sem=send, recv_sem=recv,
            device_id=device, device_id_type=MESH,
        )

    own_copy = pltpu.make_async_copy(snap_hbm, snap.at[s], sl_sem)
    own_copy.start()
    weight_copies = []
    for j in range(CHUNKS):
        part = pl.ds(j * cw, cw)
        pair = [
            pltpu.make_async_copy(wg.at[0, part], wg_v.at[part], w_sem.at[0, j]),
            pltpu.make_async_copy(wu.at[0, part], wu_v.at[part], w_sem.at[1, j]),
        ]
        weight_copies.append(pair)
        for copy in pair:
            copy.start()
    down_copies = []
    for j in range(CHUNKS):
        part = pl.ds(j * cw, cw)
        copy = pltpu.make_async_copy(wd.at[0, :, part], wd_v.at[:, part], w_sem.at[2, j])
        copy.start()
        down_copies.append(copy)

    barrier = pltpu.get_barrier_semaphore()
    for k in range(1, nz):
        pl.semaphore_signal(barrier, inc=1, device_id=(s, zpeer(k) * CORES + c), device_id_type=MESH)
    for k in range(1, ns):
        pl.semaphore_signal(barrier, inc=1, device_id=(speer(k), e), device_id_type=MESH)
    pl.semaphore_signal(barrier, inc=1, device_id=sib, device_id_type=MESH)

    zbuf[z, :, :width] = x[...]
    lane = lax.broadcasted_iota(jnp.int32, (rows, LANES), 1)
    high = jnp.zeros((rows, LANES), jnp.float32)
    low = jnp.zeros((rows, LANES), jnp.float32)
    for t in range(ids.shape[1]):
        chosen, gain = ids[:, t:t + 1], gw[:, t:t + 1]
        high = high + jnp.where(lane == chosen, gain, 0.0)
        low = low + jnp.where(lane == chosen + ne, gain, 0.0)
    low = low - low.astype(jnp.bfloat16).astype(jnp.float32)
    zbuf[z, :, width:] = jnp.where(lane < ne, high, low).astype(jnp.bfloat16)
    pl.semaphore_wait(barrier, nz + ns - 1)

    def span(j):
        return pl.ds(j * cw, cw + (LANES if j == CHUNKS - 1 else 0))

    def a1(j, k):
        piece = zbuf.at[z, :, span(j)]
        return remote(piece, piece, a1_s.at[j, k - 1], a1_r.at[j, k - 1], (s, zpeer(k) * CORES + c))

    def a2(j, k):
        piece = xs.at[c, s, :, span(j)]
        return remote(piece, piece, a2_s.at[j, k - 1], a2_r.at[j, k - 1], (speer(k), e))

    def a3(j, k):
        piece = xs.at[c, sfrom(k), :, span(j)]
        return remote(piece, piece, a3_s.at[j, k], a3_r.at[j, k], sib)

    def share(k):
        return remote(snap_hbm.at[c], snap.at[s, c], sn_s.at[k - 1], sn_r.at[k - 1], (speer(k), e))

    def forward(k):
        piece = snap.at[sfrom(k), c]
        return remote(piece, piece, sf_s.at[k - 1], sf_r.at[k - 1], sib)

    for j in range(CHUNKS):
        for k in range(1, nz):
            a1(j, k).start()

    own_f = own[...].astype(jnp.float32)
    for i in range(rows):
        part = pl.ds(i * heads, heads)
        own_score = qk_scale * jnp.sum(
            q[part, :].astype(jnp.float32) * own_f[i:i + 1], axis=1, keepdims=True
        )
        m_s[part, :] = jnp.broadcast_to(own_score, (heads, LANES))
        acc[part, :] = jnp.broadcast_to(own_f[i:i + 1, :LAT], (heads, LAT))
    l_s[...] = jnp.ones_like(l_s)

    def attend(source):
        positions = snap.shape[2]
        second = jnp.concatenate(
            [jnp.full((heads, positions), leaf[i], jnp.int32) for i in range(rows)], axis=0
        ) == 1
        keys0, keys1 = snap[source, 0], snap[source, 1]
        dims = (((1,), (1,)), ((), ()))
        queries = q[...]
        score0 = lax.dot_general(queries, keys0, dims, preferred_element_type=jnp.float32)
        score1 = lax.dot_general(queries, keys1, dims, preferred_element_type=jnp.float32)
        score = qk_scale * jnp.where(second, score1, score0)
        before = m_s[:, :1]
        now = jnp.maximum(before, jnp.max(score, axis=1, keepdims=True))
        weight = jnp.exp(score - now).astype(jnp.bfloat16).astype(jnp.float32)
        decay = jnp.exp(before - now)
        l_s[...] = l_s[...] * decay + jnp.sum(weight, axis=1, keepdims=True)
        m_s[...] = jnp.broadcast_to(now, m_s.shape)
        weight0 = jnp.where(second, 0.0, weight).astype(jnp.bfloat16)
        weight1 = jnp.where(second, weight, 0.0).astype(jnp.bfloat16)
        acc[...] = (
            acc[...] * decay
            + jnp.dot(weight0, keys0[:, :LAT], preferred_element_type=jnp.float32)
            + jnp.dot(weight1, keys1[:, :LAT], preferred_element_type=jnp.float32)
        )

    for j in range(CHUNKS):
        for k in range(1, nz):
            a1(j, k).wait_recv()
        cols = span(j)
        for i in range(nz):
            asm[i * rows:(i + 1) * rows, cols] = zbuf[i, :, cols].astype(jnp.float32)
        xs[c, s, :, cols] = asm[:, cols].astype(jnp.bfloat16)
        for k in range(1, ns):
            a2(j, k).start()
        a3(j, 0).start()
    for k in range(1, ns):
        share(k).start()

    own_copy.wait()
    attend(s)

    for j in range(CHUNKS):
        for k in range(1, ns):
            a2(j, k).wait_recv()
            a3(j, k).start()

    total = CORES * ns * nz * rows
    gate_proj = up_proj = None
    for j in range(CHUNKS):
        for k in range(ns):
            a3(j, k).wait_recv()
        for copy in weight_copies[j]:
            copy.wait()
        part = pl.ds(j * cw, cw)
        block = xs[:, :, :, part].reshape(total, cw)
        gate_j = jnp.dot(block, wg_v[part, :], preferred_element_type=jnp.float32)
        up_j = jnp.dot(block, wu_v[part, :], preferred_element_type=jnp.float32)
        gate_proj = gate_j if j == 0 else gate_proj + gate_j
        up_proj = up_j if j == 0 else up_proj + up_j
    gains = xs[:, :, :, width:].reshape(total, LANES).astype(jnp.float32)
    lane = lax.broadcasted_iota(jnp.int32, (total, LANES), 1)
    gain = jnp.sum(jnp.where((lane == e) | (lane == e + ne), gains, 0.0), axis=1, keepdims=True)
    hid[...] = (gate_proj / (1.0 + jnp.exp(-gate_proj)) * up_proj * gain).astype(jnp.bfloat16)

    def back1(j):
        return remote(pbuf.at[j, 1 - c], r1.at[j], b1_s.at[j], b1_r.at[j], sib)

    def back2(j, k):
        return remote(
            r2s.at[j, speer(k)], r2r.at[j, k - 1], b2_s.at[j, k - 1], b2_r.at[j, k - 1], (speer(k), e)
        )

    def back3(j, k):
        return remote(
            r3s.at[j, zpeer(k)], r3r.at[j, k - 1], b3_s.at[j, k - 1], b3_r.at[j, k - 1],
            (s, zpeer(k) * CORES + c),
        )

    for j in range(CHUNKS):
        down_copies[j].wait()
        partial = jnp.dot(hid[...], wd_v[:, pl.ds(j * cw, cw)], preferred_element_type=jnp.float32)
        pbuf[j] = partial.astype(jnp.bfloat16).reshape(pbuf.shape[1:])
        back1(j).start()
    for j in range(CHUNKS):
        back1(j).wait_recv()
        r2s[j] = (pbuf[j, c].astype(jnp.float32) + r1[j].astype(jnp.float32)).astype(jnp.bfloat16)
        for k in range(1, ns):
            back2(j, k).start()

    for k in range(1, ns):
        share(k).wait_recv()
        forward(k).start()

    for j in range(CHUNKS):
        mine = r2s[j, s].astype(jnp.float32)
        for k in range(1, ns):
            back2(j, k).wait_recv()
            mine = mine + r2r[j, k - 1].astype(jnp.float32)
        asm[:, pl.ds(j * cw, cw)] = mine
        for i in range(nz):
            r3s[j, i] = asm[i * rows:(i + 1) * rows, pl.ds(j * cw, cw)].astype(jnp.bfloat16)
        for k in range(1, nz):
            back3(j, k).start()

    def later(k, carry):
        forward(k).wait_recv()
        attend(sfrom(k))
        return carry

    lax.fori_loop(1, ns, later, 0)
    attn_out[...] = (acc[...] / l_s[:, :1]).astype(attn_out.dtype)

    for j in range(CHUNKS):
        mine = r3s[j, z].astype(jnp.float32)
        for k in range(1, nz):
            back3(j, k).wait_recv()
            mine = mine + r3r[j, k - 1].astype(jnp.float32)
        moe_out[:, pl.ds(j * cw, cw)] = mine.astype(moe_out.dtype)

    for j in range(CHUNKS):
        for k in range(1, nz):
            a1(j, k).wait_send()
            back3(j, k).wait_send()
        for k in range(1, ns):
            a2(j, k).wait_send()
            back2(j, k).wait_send()
        for k in range(ns):
            a3(j, k).wait_send()
        back1(j).wait_send()
    for k in range(1, ns):
        share(k).wait_send()
        forward(k).wait_send()


def body(
    queries, own_latent, snapshots, leaf_snapshot, moe_input, expert_ids, gate_weights,
    w_gate, w_up, w_down,
):
    ns, ne = lax.axis_size("seq"), lax.axis_size("exp")
    rows, heads, kdim = queries.shape
    width, ff = moe_input.shape[1], w_gate.shape[2]
    nz = ne // CORES
    group = nz * rows
    snaps, positions = snapshots.shape[:2]
    cw = width // CHUNKS
    bf16, f32 = jnp.bfloat16, jnp.float32
    vmem = pl.BlockSpec(memory_space=pltpu.VMEM)
    smem = pl.BlockSpec(memory_space=pltpu.SMEM)
    hbm = pl.BlockSpec(memory_space=pl.ANY)
    dma = pltpu.SemaphoreType.DMA
    attn, moe = pl.pallas_call(
        functools.partial(kernel, ns, ne),
        out_shape=(
            jax.ShapeDtypeStruct((rows * heads, LAT), bf16),
            jax.ShapeDtypeStruct((rows, width), bf16),
        ),
        in_specs=[vmem, vmem, hbm, smem, vmem, vmem, vmem, hbm, hbm, hbm],
        out_specs=(vmem, vmem),
        scratch_shapes=[
            pltpu.VMEM((width, ff), bf16),
            pltpu.VMEM((width, ff), bf16),
            pltpu.VMEM((ff, width), bf16),
            pltpu.VMEM((ns, snaps, positions, kdim), bf16),
            pltpu.VMEM((nz, rows, width + LANES), bf16),
            pltpu.VMEM((group, width + LANES), f32),
            pltpu.VMEM((CORES, ns, group, width + LANES), bf16),
            pltpu.VMEM((CORES * ns * group, ff), bf16),
            pltpu.VMEM((CHUNKS, CORES, ns, group, cw), bf16),
            pltpu.VMEM((CHUNKS, ns, group, cw), bf16),
            pltpu.VMEM((CHUNKS, ns, group, cw), bf16),
            pltpu.VMEM((CHUNKS, ns - 1, group, cw), bf16),
            pltpu.VMEM((CHUNKS, nz, rows, cw), bf16),
            pltpu.VMEM((CHUNKS, nz - 1, rows, cw), bf16),
            pltpu.VMEM((rows * heads, LANES), f32),
            pltpu.VMEM((rows * heads, LANES), f32),
            pltpu.VMEM((rows * heads, LAT), f32),
            dma((3, CHUNKS)),
            dma,
            dma((CHUNKS, nz - 1)), dma((CHUNKS, nz - 1)),
            dma((CHUNKS, ns - 1)), dma((CHUNKS, ns - 1)),
            dma((CHUNKS, ns)), dma((CHUNKS, ns)),
            dma((ns - 1,)), dma((ns - 1,)),
            dma((ns - 1,)), dma((ns - 1,)),
            dma((CHUNKS,)), dma((CHUNKS,)),
            dma((CHUNKS, ns - 1)), dma((CHUNKS, ns - 1)),
            dma((CHUNKS, nz - 1)), dma((CHUNKS, nz - 1)),
        ],
        compiler_params=pltpu.CompilerParams(
            collective_id=0, has_side_effects=True, vmem_limit_bytes=62 * 1024 * 1024
        ),
    )(
        queries.reshape(rows * heads, kdim), own_latent, snapshots, leaf_snapshot, moe_input,
        expert_ids, gate_weights, w_gate, w_up, w_down,
    )
    return attn.reshape(rows, heads, LAT), moe


def solution(mesh):
    in_specs = (
        P(("seq", "exp"), None, None),
        P(("seq", "exp"), None),
        P(None, "seq", None),
        P(("seq", "exp")),
        P(("seq", "exp"), None),
        P(("seq", "exp"), None),
        P(("seq", "exp"), None),
        P("exp", None, "seq"),
        P("exp", None, "seq"),
        P("exp", "seq", None),
    )
    out_specs = (P(("seq", "exp"), None, None), P(("seq", "exp"), None))
    return jax.shard_map(body, mesh=mesh, in_specs=in_specs, out_specs=out_specs, check_vma=False)
```

```python
import functools
import math

import jax
import jax.numpy as jnp
from jax import lax
from jax.experimental import pallas as pl
from jax.experimental.pallas import tpu as pltpu
from jax.sharding import PartitionSpec as P

LAT = 512
LANES = 128
CHUNKS = 2
CORES = 2
HALVES = 2
MESH = pl.DeviceIdType.MESH

qk_scale = 192.0 ** (-0.5)


def kernel(
    ns, ne, q, own, snap_hbm, leaf, x, ids, gw, wg, wu, wd, attn_out, moe_out,
    wg_v, wu_v, wd_v, snap, zbuf, asm, xs, hid, pbuf, r1, r2s, r2r, r3s, r3r, m_s, l_s, acc,
    qbuf, pick, part_s, part_r, stat_s, stat_r,
    w_sem, sl_sem, a1_s, a1_r, a2_s, a2_r, a3_s, a3_r, sn_s, sn_r, sf_s, sf_r,
    b1_s, b1_r, b2_s, b2_r, b3_s, b3_r, q_s, q_r, p_s, p_r,
):
    rows, width = x.shape
    nz = ne // CORES
    heads = q.shape[0] // rows
    cw = width // CHUNKS
    s, e = lax.axis_index("seq"), lax.axis_index("exp")
    z, c = e // CORES, e % CORES
    sib = (s, z * CORES + (1 - c))
    nx = math.isqrt(ns)
    ny = ns // nx
    sy, sx = s // nx, s % nx
    positions = snap.shape[3]
    half = positions // HALVES

    def zpeer(k):
        return lax.rem(z + k, nz)

    def speer(k):
        return lax.rem(s + k, ns)

    def sfrom(k):
        return lax.rem(s + ns - k, ns)

    def xpeer(k):
        return (sy * nx + lax.rem(sx + k, nx), e)

    def xfrom(k):
        return lax.rem(sx + nx - k, nx)

    def ypeer(k):
        return (lax.rem(sy + k, ny) * nx + sx, e)

    def yfrom(k):
        return lax.rem(sy + ny - k, ny)

    def remote(src, dst, send, recv, device):
        return pltpu.make_async_remote_copy(
            src_ref=src, dst_ref=dst, send_sem=send, recv_sem=recv,
            device_id=device, device_id_type=MESH,
        )

    own_copy = pltpu.make_async_copy(snap_hbm, snap.at[sx], sl_sem)
    own_copy.start()
    weight_copies = []
    for j in range(CHUNKS):
        part = pl.ds(j * cw, cw)
        pair = [
            pltpu.make_async_copy(wg.at[0, part], wg_v.at[part], w_sem.at[0, j]),
            pltpu.make_async_copy(wu.at[0, part], wu_v.at[part], w_sem.at[1, j]),
        ]
        weight_copies.append(pair)
        for copy in pair:
            copy.start()
    down_copies = []
    for j in range(CHUNKS):
        part = pl.ds(j * cw, cw)
        copy = pltpu.make_async_copy(wd.at[0, :, part], wd_v.at[:, part], w_sem.at[2, j])
        copy.start()
        down_copies.append(copy)

    barrier = pltpu.get_barrier_semaphore()
    for k in range(1, nz):
        pl.semaphore_signal(barrier, inc=1, device_id=(s, zpeer(k) * CORES + c), device_id_type=MESH)
    for k in range(1, ns):
        pl.semaphore_signal(barrier, inc=1, device_id=(speer(k), e), device_id_type=MESH)
    pl.semaphore_signal(barrier, inc=1, device_id=sib, device_id_type=MESH)

    zbuf[z, :, :width] = x[...]
    lane = lax.broadcasted_iota(jnp.int32, (rows, LANES), 1)
    high = jnp.zeros((rows, LANES), jnp.float32)
    low = jnp.zeros((rows, LANES), jnp.float32)
    for t in range(ids.shape[1]):
        chosen, gain = ids[:, t:t + 1], gw[:, t:t + 1]
        high = high + jnp.where(lane == chosen, gain, 0.0)
        low = low + jnp.where(lane == chosen + ne, gain, 0.0)
    low = low - low.astype(jnp.bfloat16).astype(jnp.float32)
    zbuf[z, :, width:] = jnp.where(lane < ne, high, low).astype(jnp.bfloat16)
    pl.semaphore_wait(barrier, nz + ns - 1)

    def span(j):
        return pl.ds(j * cw, cw + (LANES if j == CHUNKS - 1 else 0))

    def a1(j, k):
        piece = zbuf.at[z, :, span(j)]
        return remote(piece, piece, a1_s.at[j, k - 1], a1_r.at[j, k - 1], (s, zpeer(k) * CORES + c))

    def a2(j, k):
        piece = xs.at[c, s, :, span(j)]
        return remote(piece, piece, a2_s.at[j, k - 1], a2_r.at[j, k - 1], (speer(k), e))

    def a3(j, k):
        piece = xs.at[c, sfrom(k), :, span(j)]
        return remote(piece, piece, a3_s.at[j, k], a3_r.at[j, k], sib)

    def share(k, h):
        cols = pl.ds(h * half, half)
        return remote(
            snap_hbm.at[c, :, cols], snap.at[sx, c, :, cols], sn_s.at[k - 1, h], sn_r.at[k - 1, h], xpeer(k)
        )

    def forward(k, h):
        piece = snap.at[xfrom(k), c, :, pl.ds(h * half, half)]
        return remote(piece, piece, sf_s.at[k - 1, h], sf_r.at[k - 1, h], sib)

    def ask(k):
        return (
            remote(q, qbuf.at[k - 1], q_s.at[k - 1, 0], q_r.at[k - 1, 0], ypeer(k)),
            remote(pick.at[0], pick.at[k], q_s.at[k - 1, 1], q_r.at[k - 1, 1], ypeer(k)),
        )

    def answer(k):
        back = ypeer(ny - k)
        return (
            remote(part_s.at[k - 1], part_r.at[k - 1], p_s.at[k - 1, 0], p_r.at[k - 1, 0], back),
            remote(stat_s.at[k - 1], stat_r.at[k - 1], p_s.at[k - 1, 1], p_r.at[k - 1, 1], back),
        )

    choice = lax.broadcasted_iota(jnp.int32, pick.shape[1:], 0)
    mine = jnp.zeros(pick.shape[1:], jnp.float32)
    for i in range(rows):
        mine = jnp.where(choice == i, leaf[i].astype(jnp.float32), mine)
    pick[0] = mine

    for j in range(CHUNKS):
        for k in range(1, nz):
            a1(j, k).start()

    for k in range(1, ny):
        for copy in ask(k):
            copy.start()
    for k in range(1, nx):
        share(k, 0).start()

    own_f = own[...].astype(jnp.float32)
    for i in range(rows):
        part = pl.ds(i * heads, heads)
        own_score = qk_scale * jnp.sum(
            q[part, :].astype(jnp.float32) * own_f[i:i + 1], axis=1, keepdims=True
        )
        m_s[0, part, :] = jnp.broadcast_to(own_score, (heads, LANES))
        acc[0, part, :] = jnp.broadcast_to(own_f[i:i + 1, :LAT], (heads, LAT))
    l_s[0] = jnp.ones(l_s.shape[1:], jnp.float32)
    for k in range(1, ny):
        m_s[k] = jnp.full(m_s.shape[1:], -jnp.inf, jnp.float32)
        l_s[k] = jnp.zeros(l_s.shape[1:], jnp.float32)
        acc[k] = jnp.zeros(acc.shape[1:], jnp.float32)

    def attend(group, source):
        second = jnp.concatenate(
            [jnp.broadcast_to(pick[group, i:i + 1, :1], (heads, positions)) for i in range(rows)], axis=0
        ) > 0.5
        keys0, keys1 = snap[source, 0], snap[source, 1]
        queries = q[...] if group == 0 else qbuf[group - 1]
        score0 = jnp.dot(queries, keys0, preferred_element_type=jnp.float32)
        score1 = jnp.dot(queries, keys1, preferred_element_type=jnp.float32)
        score = qk_scale * jnp.where(second, score1, score0)
        before = m_s[group, :, :1]
        now = jnp.maximum(before, jnp.max(score, axis=1, keepdims=True))
        weight = jnp.exp(score - now).astype(jnp.bfloat16).astype(jnp.float32)
        decay = jnp.exp(before - now)
        l_s[group] = l_s[group] * decay + jnp.sum(weight, axis=1, keepdims=True)
        m_s[group] = jnp.broadcast_to(now, m_s.shape[1:])
        weight0 = jnp.where(second, 0.0, weight).astype(jnp.bfloat16)
        weight1 = jnp.where(second, weight, 0.0).astype(jnp.bfloat16)
        dims = (((1,), (1,)), ((), ()))
        acc[group] = (
            acc[group] * decay
            + lax.dot_general(weight0, keys0[:LAT], dims, preferred_element_type=jnp.float32)
            + lax.dot_general(weight1, keys1[:LAT], dims, preferred_element_type=jnp.float32)
        )

    for j in range(CHUNKS):
        for k in range(1, nz):
            a1(j, k).wait_recv()
        cols = span(j)
        for i in range(nz):
            asm[i * rows:(i + 1) * rows, cols] = zbuf[i, :, cols].astype(jnp.float32)
        xs[c, s, :, cols] = asm[:, cols].astype(jnp.bfloat16)
        for k in range(1, ns):
            a2(j, k).start()
        a3(j, 0).start()
    for k in range(1, nx):
        for h in range(1, HALVES):
            share(k, h).start()

    own_copy.wait()
    attend(0, sx)
    for k in range(1, ny):
        for copy in ask(k):
            copy.wait_recv()
        attend(k, sx)

    for j in range(CHUNKS):
        for k in range(1, ns):
            a2(j, k).wait_recv()
            a3(j, k).start()
    for k in range(1, nx):
        share(k, 0).wait_recv()
        forward(k, 0).start()

    total = CORES * ns * nz * rows
    gate_proj = up_proj = None
    for j in range(CHUNKS):
        for k in range(ns):
            a3(j, k).wait_recv()
        for copy in weight_copies[j]:
            copy.wait()
        part = pl.ds(j * cw, cw)
        block = xs[:, :, :, part].reshape(total, cw)
        gate_j = jnp.dot(block, wg_v[part, :], preferred_element_type=jnp.float32)
        up_j = jnp.dot(block, wu_v[part, :], preferred_element_type=jnp.float32)
        gate_proj = gate_j if j == 0 else gate_proj + gate_j
        up_proj = up_j if j == 0 else up_proj + up_j
    gains = xs[:, :, :, width:].reshape(total, LANES).astype(jnp.float32)
    lane = lax.broadcasted_iota(jnp.int32, (total, LANES), 1)
    gain = jnp.sum(jnp.where((lane == e) | (lane == e + ne), gains, 0.0), axis=1, keepdims=True)
    hid[...] = (gate_proj / (1.0 + jnp.exp(-gate_proj)) * up_proj * gain).astype(jnp.bfloat16)

    def back1(j):
        return remote(pbuf.at[j, 1 - c], r1.at[j], b1_s.at[j], b1_r.at[j], sib)

    def back2(j, k):
        return remote(
            r2s.at[j, speer(k)], r2r.at[j, k - 1], b2_s.at[j, k - 1], b2_r.at[j, k - 1], (speer(k), e)
        )

    def back3(j, k):
        return remote(
            r3s.at[j, zpeer(k)], r3r.at[j, k - 1], b3_s.at[j, k - 1], b3_r.at[j, k - 1],
            (s, zpeer(k) * CORES + c),
        )

    for j in range(CHUNKS):
        down_copies[j].wait()
        partial = jnp.dot(hid[...], wd_v[:, pl.ds(j * cw, cw)], preferred_element_type=jnp.float32)
        pbuf[j] = partial.astype(jnp.bfloat16).reshape(pbuf.shape[1:])
        back1(j).start()
    for j in range(CHUNKS):
        back1(j).wait_recv()
        r2s[j] = (pbuf[j, c].astype(jnp.float32) + r1[j].astype(jnp.float32)).astype(jnp.bfloat16)
        for k in range(1, ns):
            back2(j, k).start()

    for k in range(1, nx):
        for h in range(1, HALVES):
            share(k, h).wait_recv()
            forward(k, h).start()
    for k in range(1, nx):
        for h in range(HALVES):
            forward(k, h).wait_recv()
    lane = lax.broadcasted_iota(jnp.int32, m_s.shape[1:], 1)
    for g in range(1, ny):
        def later(k, carry, g=g):
            attend(g, xfrom(k))
            return carry

        lax.fori_loop(1, nx, later, 0)
        part_s[g - 1] = acc[g].astype(jnp.bfloat16)
        stat_s[g - 1] = jnp.where(lane == 0, m_s[g], l_s[g]).T[:stat_s.shape[1]]
        for copy in answer(g):
            copy.start()

    for j in range(CHUNKS):
        mine = r2s[j, s].astype(jnp.float32)
        for k in range(1, ns):
            back2(j, k).wait_recv()
            mine = mine + r2r[j, k - 1].astype(jnp.float32)
        asm[:, pl.ds(j * cw, cw)] = mine
        for i in range(nz):
            r3s[j, i] = asm[i * rows:(i + 1) * rows, pl.ds(j * cw, cw)].astype(jnp.bfloat16)
        for k in range(1, nz):
            back3(j, k).start()

    def last(k, carry):
        attend(0, xfrom(k))
        return carry

    lax.fori_loop(1, nx, last, 0)
    top, mass, value = m_s[0, :, :1], l_s[0, :, :1], acc[0]
    for k in range(1, ny):
        for copy in answer(k):
            copy.wait_recv()
        blank = jnp.zeros((LANES - stat_r.shape[1], stat_r.shape[2]), jnp.float32)
        stats = jnp.concatenate([stat_r[k - 1], blank], axis=0).T
        other = stats[:, :1]
        now = jnp.maximum(top, other)
        mine, theirs = jnp.exp(top - now), jnp.exp(other - now)
        mass = mass * mine + stats[:, 1:2] * theirs
        value = value * mine + part_r[k - 1].astype(jnp.float32) * theirs
        top = now
    attn_out[...] = (value / mass).astype(attn_out.dtype)

    for j in range(CHUNKS):
        mine = r3s[j, z].astype(jnp.float32)
        for k in range(1, nz):
            back3(j, k).wait_recv()
            mine = mine + r3r[j, k - 1].astype(jnp.float32)
        moe_out[:, pl.ds(j * cw, cw)] = mine.astype(moe_out.dtype)

    for j in range(CHUNKS):
        for k in range(1, nz):
            a1(j, k).wait_send()
            back3(j, k).wait_send()
        for k in range(1, ns):
            a2(j, k).wait_send()
            back2(j, k).wait_send()
        for k in range(ns):
            a3(j, k).wait_send()
        back1(j).wait_send()
    for k in range(1, nx):
        for h in range(HALVES):
            share(k, h).wait_send()
            forward(k, h).wait_send()
    for k in range(1, ny):
        for copy in ask(k) + answer(k):
            copy.wait_send()


def body(
    queries, own_latent, snapshots, leaf_snapshot, moe_input, expert_ids, gate_weights,
    w_gate, w_up, w_down,
):
    ns, ne = lax.axis_size("seq"), lax.axis_size("exp")
    rows, heads, kdim = queries.shape
    width, ff = moe_input.shape[1], w_gate.shape[2]
    nz = ne // CORES
    group = nz * rows
    snaps, positions = snapshots.shape[:2]
    nx = math.isqrt(ns)
    ny = ns // nx
    assert nx * ny == ns and ny > 1
    lines = rows * heads
    cw = width // CHUNKS
    bf16, f32 = jnp.bfloat16, jnp.float32
    vmem = pl.BlockSpec(memory_space=pltpu.VMEM)
    smem = pl.BlockSpec(memory_space=pltpu.SMEM)
    hbm = pl.BlockSpec(memory_space=pl.ANY)
    dma = pltpu.SemaphoreType.DMA
    attn, moe = pl.pallas_call(
        functools.partial(kernel, ns, ne),
        out_shape=(
            jax.ShapeDtypeStruct((rows * heads, LAT), bf16),
            jax.ShapeDtypeStruct((rows, width), bf16),
        ),
        in_specs=[vmem, vmem, hbm, smem, vmem, vmem, vmem, hbm, hbm, hbm],
        out_specs=(vmem, vmem),
        scratch_shapes=[
            pltpu.VMEM((width, ff), bf16),
            pltpu.VMEM((width, ff), bf16),
            pltpu.VMEM((ff, width), bf16),
            pltpu.VMEM((nx, snaps, kdim, positions), bf16),
            pltpu.VMEM((nz, rows, width + LANES), bf16),
            pltpu.VMEM((group, width + LANES), f32),
            pltpu.VMEM((CORES, ns, group, width + LANES), bf16),
            pltpu.VMEM((CORES * ns * group, ff), bf16),
            pltpu.VMEM((CHUNKS, CORES, ns, group, cw), bf16),
            pltpu.VMEM((CHUNKS, ns, group, cw), bf16),
            pltpu.VMEM((CHUNKS, ns, group, cw), bf16),
            pltpu.VMEM((CHUNKS, ns - 1, group, cw), bf16),
            pltpu.VMEM((CHUNKS, nz, rows, cw), bf16),
            pltpu.VMEM((CHUNKS, nz - 1, rows, cw), bf16),
            pltpu.VMEM((ny, lines, LANES), f32),
            pltpu.VMEM((ny, lines, LANES), f32),
            pltpu.VMEM((ny, lines, LAT), f32),
            pltpu.VMEM((ny - 1, lines, kdim), bf16),
            pltpu.VMEM((ny, 8, LANES), f32),
            pltpu.VMEM((ny - 1, lines, LAT), bf16),
            pltpu.VMEM((ny - 1, lines, LAT), bf16),
            pltpu.VMEM((ny - 1, 8, lines), f32),
            pltpu.VMEM((ny - 1, 8, lines), f32),
            dma((3, CHUNKS)),
            dma,
            dma((CHUNKS, nz - 1)), dma((CHUNKS, nz - 1)),
            dma((CHUNKS, ns - 1)), dma((CHUNKS, ns - 1)),
            dma((CHUNKS, ns)), dma((CHUNKS, ns)),
            dma((nx - 1, HALVES)), dma((nx - 1, HALVES)),
            dma((nx - 1, HALVES)), dma((nx - 1, HALVES)),
            dma((CHUNKS,)), dma((CHUNKS,)),
            dma((CHUNKS, ns - 1)), dma((CHUNKS, ns - 1)),
            dma((CHUNKS, nz - 1)), dma((CHUNKS, nz - 1)),
            dma((ny - 1, 2)), dma((ny - 1, 2)),
            dma((ny - 1, 2)), dma((ny - 1, 2)),
        ],
        compiler_params=pltpu.CompilerParams(
            collective_id=0, has_side_effects=True, vmem_limit_bytes=62 * 1024 * 1024
        ),
    )(
        queries.reshape(rows * heads, kdim), own_latent, jnp.swapaxes(snapshots, 1, 2), leaf_snapshot,
        moe_input, expert_ids, gate_weights, w_gate, w_up, w_down,
    )
    return attn.reshape(rows, heads, LAT), moe


def solution(mesh):
    in_specs = (
        P(("seq", "exp"), None, None),
        P(("seq", "exp"), None),
        P(None, "seq", None),
        P(("seq", "exp")),
        P(("seq", "exp"), None),
        P(("seq", "exp"), None),
        P(("seq", "exp"), None),
        P("exp", None, "seq"),
        P("exp", None, "seq"),
        P("exp", "seq", None),
    )
    out_specs = (P(("seq", "exp"), None, None), P(("seq", "exp"), None))
    return jax.shard_map(body, mesh=mesh, in_specs=in_specs, out_specs=out_specs, check_vma=False)
```

```python
import functools
import math

import jax
import jax.numpy as jnp
from jax import lax
from jax.experimental import pallas as pl
from jax.experimental.pallas import tpu as pltpu
from jax.sharding import PartitionSpec as P

LAT = 512
LANES = 128
CHUNKS = 4
CORES = 2
HALVES = 2
MESH = pl.DeviceIdType.MESH

qk_scale = 192.0 ** (-0.5)


def kernel(
    ns, ne, q, own, snap_hbm, leaf, x, ids, gw, wg, wu, wd, attn_out, moe_out,
    wg_v, wu_v, wd_v, snap, zbuf, asm, xs, hid, pbuf, r1, r2s, r2r, r3s, r3r, m_s, l_s, acc,
    qbuf, pick, part_s, part_r, stat_s, stat_r,
    w_sem, sl_sem, a1_s, a1_r, a2_s, a2_r, a3_s, a3_r, sn_s, sn_r, sf_s, sf_r,
    b1_s, b1_r, b2_s, b2_r, b3_s, b3_r, q_s, q_r, p_s, p_r,
):
    rows, width = x.shape
    nz = ne // CORES
    heads = q.shape[0] // rows
    cw = width // CHUNKS
    s, e = lax.axis_index("seq"), lax.axis_index("exp")
    z, c = e // CORES, e % CORES
    sib = (s, z * CORES + (1 - c))
    nx = math.isqrt(ns)
    ny = ns // nx
    sy, sx = s // nx, s % nx
    positions = snap.shape[3]
    half = positions // HALVES

    def zpeer(k):
        return lax.rem(z + k, nz)

    def speer(k):
        return lax.rem(s + k, ns)

    def xpeer(k):
        return (sy * nx + lax.rem(sx + k, nx), e)

    def xfrom(k):
        return lax.rem(sx + nx - k, nx)

    def ypeer(k):
        return (lax.rem(sy + k, ny) * nx + sx, e)

    def yfrom(k):
        return lax.rem(sy + ny - k, ny)

    def remote(src, dst, send, recv, device):
        return pltpu.make_async_remote_copy(
            src_ref=src, dst_ref=dst, send_sem=send, recv_sem=recv,
            device_id=device, device_id_type=MESH,
        )

    own_copy = pltpu.make_async_copy(snap_hbm, snap.at[sx], sl_sem)
    own_copy.start()
    weight_copies = []
    for j in range(CHUNKS):
        part = pl.ds(j * cw, cw)
        pair = [
            pltpu.make_async_copy(wg.at[0, part], wg_v.at[part], w_sem.at[0, j]),
            pltpu.make_async_copy(wu.at[0, part], wu_v.at[part], w_sem.at[1, j]),
        ]
        weight_copies.append(pair)
        for copy in pair:
            copy.start()
    down_copies = []
    for j in range(CHUNKS):
        part = pl.ds(j * cw, cw)
        copy = pltpu.make_async_copy(wd.at[0, :, part], wd_v.at[:, part], w_sem.at[2, j])
        copy.start()
        down_copies.append(copy)

    barrier = pltpu.get_barrier_semaphore()
    for k in range(1, nz):
        pl.semaphore_signal(barrier, inc=1, device_id=(s, zpeer(k) * CORES + c), device_id_type=MESH)
    for k in range(1, ns):
        pl.semaphore_signal(barrier, inc=1, device_id=(speer(k), e), device_id_type=MESH)
    pl.semaphore_signal(barrier, inc=1, device_id=sib, device_id_type=MESH)

    zbuf[z, :, :width] = x[...]
    lane = lax.broadcasted_iota(jnp.int32, (rows, LANES), 1)
    high = jnp.zeros((rows, LANES), jnp.float32)
    low = jnp.zeros((rows, LANES), jnp.float32)
    for t in range(ids.shape[1]):
        chosen, gain = ids[:, t:t + 1], gw[:, t:t + 1]
        high = high + jnp.where(lane == chosen, gain, 0.0)
        low = low + jnp.where(lane == chosen + ne, gain, 0.0)
    low = low - low.astype(jnp.bfloat16).astype(jnp.float32)
    zbuf[z, :, width:] = jnp.where(lane < ne, high, low).astype(jnp.bfloat16)
    pl.semaphore_wait(barrier, nz + ns - 1)

    def span(j):
        return pl.ds(j * cw, cw + (LANES if j == CHUNKS - 1 else 0))

    def a1(j, k):
        piece = zbuf.at[z, :, span(j)]
        return remote(piece, piece, a1_s.at[j, k - 1], a1_r.at[j, k - 1], (s, zpeer(k) * CORES + c))

    def source(k):
        return lax.rem(sy + ny - k // nx, ny) * nx + lax.rem(sx + nx - k % nx, nx)

    def xfirst(j):
        return j % 2 == 0

    def steps(j):
        ahead, beside = list(range(1, nx)), list(range(nx, ns, nx))
        return (ahead, beside) if xfirst(j) else (beside, ahead)

    def a2(j, k, d):
        piece = xs.at[c, source(k), :, span(j)]
        to = xpeer(d) if d < nx else ypeer(d // nx)
        return remote(piece, piece, a2_s.at[j, k + d - 1], a2_r.at[j, k + d - 1], to)

    def a2_wait(j, k):
        piece = xs.at[c, source(k), :, span(j)]
        remote(piece, piece, a2_s.at[j, k - 1], a2_r.at[j, k - 1], xpeer(1)).wait_recv()

    def a2_sent(j, k):
        piece = xs.at[c, source(k), :, span(j)]
        remote(piece, piece, a2_s.at[j, k - 1], a2_r.at[j, k - 1], xpeer(1)).wait_send()

    def a3(j, k):
        piece = xs.at[c, source(k), :, span(j)]
        return remote(piece, piece, a3_s.at[j, k], a3_r.at[j, k], sib)

    def share(k, h):
        cols = pl.ds(h * half, half)
        return remote(
            snap_hbm.at[c, :, cols], snap.at[sx, c, :, cols], sn_s.at[k - 1, h], sn_r.at[k - 1, h], xpeer(k)
        )

    def forward(k, h):
        piece = snap.at[xfrom(k), c, :, pl.ds(h * half, half)]
        return remote(piece, piece, sf_s.at[k - 1, h], sf_r.at[k - 1, h], sib)

    def ask(k):
        return (
            remote(q, qbuf.at[k - 1], q_s.at[k - 1, 0], q_r.at[k - 1, 0], ypeer(k)),
            remote(pick.at[0], pick.at[k], q_s.at[k - 1, 1], q_r.at[k - 1, 1], ypeer(k)),
        )

    def answer(k):
        back = ypeer(ny - k)
        return (
            remote(part_s.at[k - 1], part_r.at[k - 1], p_s.at[k - 1, 0], p_r.at[k - 1, 0], back),
            remote(stat_s.at[k - 1], stat_r.at[k - 1], p_s.at[k - 1, 1], p_r.at[k - 1, 1], back),
        )

    choice = lax.broadcasted_iota(jnp.int32, pick.shape[1:], 0)
    mine = jnp.zeros(pick.shape[1:], jnp.float32)
    for i in range(rows):
        mine = jnp.where(choice == i, leaf[i].astype(jnp.float32), mine)
    pick[0] = mine

    for j in range(CHUNKS):
        for k in range(1, nz):
            a1(j, k).start()

    for k in range(1, ny):
        for copy in ask(k):
            copy.start()
    for k in range(1, nx):
        share(k, 0).start()

    own_f = own[...].astype(jnp.float32)
    for i in range(rows):
        part = pl.ds(i * heads, heads)
        own_score = qk_scale * jnp.sum(
            q[part, :].astype(jnp.float32) * own_f[i:i + 1], axis=1, keepdims=True
        )
        m_s[0, part, :] = jnp.broadcast_to(own_score, (heads, LANES))
        acc[0, part, :] = jnp.broadcast_to(own_f[i:i + 1, :LAT], (heads, LAT))
    l_s[0] = jnp.ones(l_s.shape[1:], jnp.float32)
    for k in range(1, ny):
        m_s[k] = jnp.full(m_s.shape[1:], -jnp.inf, jnp.float32)
        l_s[k] = jnp.zeros(l_s.shape[1:], jnp.float32)
        acc[k] = jnp.zeros(acc.shape[1:], jnp.float32)

    def attend(group, source):
        second = jnp.concatenate(
            [jnp.broadcast_to(pick[group, i:i + 1, :1], (heads, positions)) for i in range(rows)], axis=0
        ) > 0.5
        keys0, keys1 = snap[source, 0], snap[source, 1]
        queries = q[...] if group == 0 else qbuf[group - 1]
        score0 = jnp.dot(queries, keys0, preferred_element_type=jnp.float32)
        score1 = jnp.dot(queries, keys1, preferred_element_type=jnp.float32)
        score = qk_scale * jnp.where(second, score1, score0)
        before = m_s[group, :, :1]
        now = jnp.maximum(before, jnp.max(score, axis=1, keepdims=True))
        weight = jnp.exp(score - now).astype(jnp.bfloat16).astype(jnp.float32)
        decay = jnp.exp(before - now)
        l_s[group] = l_s[group] * decay + jnp.sum(weight, axis=1, keepdims=True)
        m_s[group] = jnp.broadcast_to(now, m_s.shape[1:])
        weight0 = jnp.where(second, 0.0, weight).astype(jnp.bfloat16)
        weight1 = jnp.where(second, weight, 0.0).astype(jnp.bfloat16)
        dims = (((1,), (1,)), ((), ()))
        acc[group] = (
            acc[group] * decay
            + lax.dot_general(weight0, keys0[:LAT], dims, preferred_element_type=jnp.float32)
            + lax.dot_general(weight1, keys1[:LAT], dims, preferred_element_type=jnp.float32)
        )

    own_copy.wait()
    attend(0, sx)

    for j in range(CHUNKS):
        for k in range(1, nz):
            a1(j, k).wait_recv()
        cols = span(j)
        for i in range(nz):
            asm[i * rows:(i + 1) * rows, cols] = zbuf[i, :, cols].astype(jnp.float32)
        xs[c, s, :, cols] = asm[:, cols].astype(jnp.bfloat16)
        first, second_step = steps(j)
        for d in first + second_step:
            a2(j, 0, d).start()
        a3(j, 0).start()

    for j in range(CHUNKS):
        first, second_step = steps(j)
        for k in first:
            a2_wait(j, k)
            for d in second_step:
                a2(j, k, d).start()
            a3(j, k).start()
    for k in range(1, ny):
        for copy in ask(k):
            copy.wait_recv()
        attend(k, sx)

    total = CORES * ns * nz * rows

    def project(j, sums):
        for k in range(ns):
            a3(j, k).wait_recv()
        for copy in weight_copies[j]:
            copy.wait()
        part = pl.ds(j * cw, cw)
        block = xs[:, :, :, part].reshape(total, cw)
        gate_j = jnp.dot(block, wg_v[part, :], preferred_element_type=jnp.float32)
        up_j = jnp.dot(block, wu_v[part, :], preferred_element_type=jnp.float32)
        return (gate_j, up_j) if sums is None else (sums[0] + gate_j, sums[1] + up_j)

    sums = None
    for j in range(CHUNKS):
        first, _ = steps(j)
        for k in range(1, ns):
            if k not in first:
                a2_wait(j, k)
                a3(j, k).start()
        if j == CHUNKS - 1:
            for k in range(1, nx):
                for h in range(1, HALVES):
                    share(k, h).start()
                share(k, 0).wait_recv()
                forward(k, 0).start()
        if j >= 1:
            sums = project(j - 1, sums)
    gate_proj, up_proj = project(CHUNKS - 1, sums)
    gains = xs[:, :, :, width:].reshape(total, LANES).astype(jnp.float32)
    lane = lax.broadcasted_iota(jnp.int32, (total, LANES), 1)
    gain = jnp.sum(jnp.where((lane == e) | (lane == e + ne), gains, 0.0), axis=1, keepdims=True)
    hid[...] = (gate_proj / (1.0 + jnp.exp(-gate_proj)) * up_proj * gain).astype(jnp.bfloat16)

    def back1(j):
        return remote(pbuf.at[j, 1 - c], r1.at[j], b1_s.at[j], b1_r.at[j], sib)

    def back2(j, k):
        return remote(
            r2s.at[j, speer(k)], r2r.at[j, k - 1], b2_s.at[j, k - 1], b2_r.at[j, k - 1], (speer(k), e)
        )

    def back3(j, k):
        return remote(
            r3s.at[j, zpeer(k)], r3r.at[j, k - 1], b3_s.at[j, k - 1], b3_r.at[j, k - 1],
            (s, zpeer(k) * CORES + c),
        )

    def spread(j):
        back1(j).wait_recv()
        r2s[j] = (pbuf[j, c].astype(jnp.float32) + r1[j].astype(jnp.float32)).astype(jnp.bfloat16)
        for k in range(1, ns):
            back2(j, k).start()

    for j in range(CHUNKS):
        down_copies[j].wait()
        partial = jnp.dot(hid[...], wd_v[:, pl.ds(j * cw, cw)], preferred_element_type=jnp.float32)
        pbuf[j] = partial.astype(jnp.bfloat16).reshape(pbuf.shape[1:])
        back1(j).start()
        if j >= 1:
            spread(j - 1)
    spread(CHUNKS - 1)

    for k in range(1, nx):
        for h in range(1, HALVES):
            share(k, h).wait_recv()
            forward(k, h).start()
    for k in range(1, nx):
        for h in range(HALVES):
            forward(k, h).wait_recv()
    lane = lax.broadcasted_iota(jnp.int32, m_s.shape[1:], 1)
    for g in range(1, ny):
        def later(k, carry, g=g):
            attend(g, xfrom(k))
            return carry

        lax.fori_loop(1, nx, later, 0)
        part_s[g - 1] = acc[g].astype(jnp.bfloat16)
        stat_s[g - 1] = jnp.where(lane == 0, m_s[g], l_s[g]).T[:stat_s.shape[1]]
        for copy in answer(g):
            copy.start()

    for j in range(CHUNKS):
        mine = r2s[j, s].astype(jnp.float32)
        for k in range(1, ns):
            back2(j, k).wait_recv()
            mine = mine + r2r[j, k - 1].astype(jnp.float32)
        asm[:, pl.ds(j * cw, cw)] = mine
        for i in range(nz):
            r3s[j, i] = asm[i * rows:(i + 1) * rows, pl.ds(j * cw, cw)].astype(jnp.bfloat16)
        for k in range(1, nz):
            back3(j, k).start()

    def last(k, carry):
        attend(0, xfrom(k))
        return carry

    lax.fori_loop(1, nx, last, 0)
    top, mass, value = m_s[0, :, :1], l_s[0, :, :1], acc[0]
    for k in range(1, ny):
        for copy in answer(k):
            copy.wait_recv()
        blank = jnp.zeros((LANES - stat_r.shape[1], stat_r.shape[2]), jnp.float32)
        stats = jnp.concatenate([stat_r[k - 1], blank], axis=0).T
        other = stats[:, :1]
        now = jnp.maximum(top, other)
        mine, theirs = jnp.exp(top - now), jnp.exp(other - now)
        mass = mass * mine + stats[:, 1:2] * theirs
        value = value * mine + part_r[k - 1].astype(jnp.float32) * theirs
        top = now
    attn_out[...] = (value / mass).astype(attn_out.dtype)

    for j in range(CHUNKS):
        mine = r3s[j, z].astype(jnp.float32)
        for k in range(1, nz):
            back3(j, k).wait_recv()
            mine = mine + r3r[j, k - 1].astype(jnp.float32)
        moe_out[:, pl.ds(j * cw, cw)] = mine.astype(moe_out.dtype)

    for j in range(CHUNKS):
        for k in range(1, nz):
            a1(j, k).wait_send()
            back3(j, k).wait_send()
        for k in range(1, ns):
            a2_sent(j, k)
            back2(j, k).wait_send()
        for k in range(ns):
            a3(j, k).wait_send()
        back1(j).wait_send()
    for k in range(1, nx):
        for h in range(HALVES):
            share(k, h).wait_send()
            forward(k, h).wait_send()
    for k in range(1, ny):
        for copy in ask(k) + answer(k):
            copy.wait_send()


def body(
    queries, own_latent, snapshots, leaf_snapshot, moe_input, expert_ids, gate_weights,
    w_gate, w_up, w_down,
):
    ns, ne = lax.axis_size("seq"), lax.axis_size("exp")
    rows, heads, kdim = queries.shape
    width, ff = moe_input.shape[1], w_gate.shape[2]
    nz = ne // CORES
    group = nz * rows
    snaps, positions = snapshots.shape[:2]
    nx = math.isqrt(ns)
    ny = ns // nx
    assert nx * ny == ns and ny > 1
    lines = rows * heads
    cw = width // CHUNKS
    bf16, f32 = jnp.bfloat16, jnp.float32
    vmem = pl.BlockSpec(memory_space=pltpu.VMEM)
    smem = pl.BlockSpec(memory_space=pltpu.SMEM)
    hbm = pl.BlockSpec(memory_space=pl.ANY)
    dma = pltpu.SemaphoreType.DMA
    attn, moe = pl.pallas_call(
        functools.partial(kernel, ns, ne),
        out_shape=(
            jax.ShapeDtypeStruct((rows * heads, LAT), bf16),
            jax.ShapeDtypeStruct((rows, width), bf16),
        ),
        in_specs=[vmem, vmem, hbm, smem, vmem, vmem, vmem, hbm, hbm, hbm],
        out_specs=(vmem, vmem),
        scratch_shapes=[
            pltpu.VMEM((width, ff), bf16),
            pltpu.VMEM((width, ff), bf16),
            pltpu.VMEM((ff, width), bf16),
            pltpu.VMEM((nx, snaps, kdim, positions), bf16),
            pltpu.VMEM((nz, rows, width + LANES), bf16),
            pltpu.VMEM((group, width + LANES), f32),
            pltpu.VMEM((CORES, ns, group, width + LANES), bf16),
            pltpu.VMEM((CORES * ns * group, ff), bf16),
            pltpu.VMEM((CHUNKS, CORES, ns, group, cw), bf16),
            pltpu.VMEM((CHUNKS, ns, group, cw), bf16),
            pltpu.VMEM((CHUNKS, ns, group, cw), bf16),
            pltpu.VMEM((CHUNKS, ns - 1, group, cw), bf16),
            pltpu.VMEM((CHUNKS, nz, rows, cw), bf16),
            pltpu.VMEM((CHUNKS, nz - 1, rows, cw), bf16),
            pltpu.VMEM((ny, lines, LANES), f32),
            pltpu.VMEM((ny, lines, LANES), f32),
            pltpu.VMEM((ny, lines, LAT), f32),
            pltpu.VMEM((ny - 1, lines, kdim), bf16),
            pltpu.VMEM((ny, 8, LANES), f32),
            pltpu.VMEM((ny - 1, lines, LAT), bf16),
            pltpu.VMEM((ny - 1, lines, LAT), bf16),
            pltpu.VMEM((ny - 1, 8, lines), f32),
            pltpu.VMEM((ny - 1, 8, lines), f32),
            dma((3, CHUNKS)),
            dma,
            dma((CHUNKS, nz - 1)), dma((CHUNKS, nz - 1)),
            dma((CHUNKS, ns - 1)), dma((CHUNKS, ns - 1)),
            dma((CHUNKS, ns)), dma((CHUNKS, ns)),
            dma((nx - 1, HALVES)), dma((nx - 1, HALVES)),
            dma((nx - 1, HALVES)), dma((nx - 1, HALVES)),
            dma((CHUNKS,)), dma((CHUNKS,)),
            dma((CHUNKS, ns - 1)), dma((CHUNKS, ns - 1)),
            dma((CHUNKS, nz - 1)), dma((CHUNKS, nz - 1)),
            dma((ny - 1, 2)), dma((ny - 1, 2)),
            dma((ny - 1, 2)), dma((ny - 1, 2)),
        ],
        compiler_params=pltpu.CompilerParams(
            collective_id=0, has_side_effects=True, vmem_limit_bytes=62 * 1024 * 1024
        ),
    )(
        queries.reshape(rows * heads, kdim), own_latent, jnp.swapaxes(snapshots, 1, 2), leaf_snapshot,
        moe_input, expert_ids, gate_weights, w_gate, w_up, w_down,
    )
    return attn.reshape(rows, heads, LAT), moe


def solution(mesh):
    in_specs = (
        P(("seq", "exp"), None, None),
        P(("seq", "exp"), None),
        P(None, "seq", None),
        P(("seq", "exp")),
        P(("seq", "exp"), None),
        P(("seq", "exp"), None),
        P(("seq", "exp"), None),
        P("exp", None, "seq"),
        P("exp", None, "seq"),
        P("exp", "seq", None),
    )
    out_specs = (P(("seq", "exp"), None, None), P(("seq", "exp"), None))
    return jax.shard_map(body, mesh=mesh, in_specs=in_specs, out_specs=out_specs, check_vma=False)
```

```python
import functools
import math

import jax
import jax.numpy as jnp
from jax import lax
from jax.experimental import pallas as pl
from jax.experimental.pallas import tpu as pltpu
from jax.sharding import PartitionSpec as P

LAT = 512
LANES = 128
CHUNKS = 4
CORES = 2
PIECES = 2
MESH = pl.DeviceIdType.MESH

qk_scale = 192.0 ** (-0.5)


def kernel(
    ns, ne, q, own, snap_hbm, leaf, x, ids, gw, wg, wu, wd, attn_out, moe_out,
    wg_v, wu_v, wd_v, snap, zbuf, asm, xs, hid, pbuf, r1, r2s, r2r, r3s, r3r, m_s, l_s, acc,
    qbuf, pick, part_s, part_r, stat_s, stat_r,
    w_sem, sl_sem, a1_s, a1_r, a2_s, a2_r, a3_s, a3_r, sn_s, sn_r, sz_s, sz_r, sf_s, sf_r,
    b1_s, b1_r, b2_s, b2_r, b3_s, b3_r, q_s, q_r, p_s, p_r,
):
    rows, width = x.shape
    nz = ne // CORES
    heads = q.shape[0] // rows
    cw = width // CHUNKS
    s, e = lax.axis_index("seq"), lax.axis_index("exp")
    z, c = e // CORES, e % CORES
    sib = (s, z * CORES + (1 - c))
    nx = math.isqrt(ns)
    ny = ns // nx
    sy, sx = s // nx, s % nx
    positions = snap.shape[3]
    size = positions // (2 * PIECES)
    plane = z % 2
    other_plane = (s, (z + 1 - 2 * plane) * CORES + c)

    def zpeer(k):
        return lax.rem(z + k, nz)

    def speer(k):
        return lax.rem(s + k, ns)

    def xpeer(k):
        return (sy * nx + lax.rem(sx + k, nx), e)

    def xfrom(k):
        return lax.rem(sx + nx - k, nx)

    def ypeer(k):
        return (lax.rem(sy + k, ny) * nx + sx, e)

    def yfrom(k):
        return lax.rem(sy + ny - k, ny)

    def remote(src, dst, send, recv, device):
        return pltpu.make_async_remote_copy(
            src_ref=src, dst_ref=dst, send_sem=send, recv_sem=recv,
            device_id=device, device_id_type=MESH,
        )

    own_copy = pltpu.make_async_copy(snap_hbm, snap.at[sx], sl_sem)
    own_copy.start()
    weight_copies = []
    for j in range(CHUNKS):
        part = pl.ds(j * cw, cw)
        pair = [
            pltpu.make_async_copy(wg.at[0, part], wg_v.at[part], w_sem.at[0, j]),
            pltpu.make_async_copy(wu.at[0, part], wu_v.at[part], w_sem.at[1, j]),
        ]
        weight_copies.append(pair)
        for copy in pair:
            copy.start()
    down_copies = []
    for j in range(CHUNKS):
        part = pl.ds(j * cw, cw)
        copy = pltpu.make_async_copy(wd.at[0, :, part], wd_v.at[:, part], w_sem.at[2, j])
        copy.start()
        down_copies.append(copy)

    barrier = pltpu.get_barrier_semaphore()
    for k in range(1, nz):
        pl.semaphore_signal(barrier, inc=1, device_id=(s, zpeer(k) * CORES + c), device_id_type=MESH)
    for k in range(1, ns):
        pl.semaphore_signal(barrier, inc=1, device_id=(speer(k), e), device_id_type=MESH)
    pl.semaphore_signal(barrier, inc=1, device_id=sib, device_id_type=MESH)

    zbuf[z, :, :width] = x[...]
    lane = lax.broadcasted_iota(jnp.int32, (rows, LANES), 1)
    high = jnp.zeros((rows, LANES), jnp.float32)
    low = jnp.zeros((rows, LANES), jnp.float32)
    for t in range(ids.shape[1]):
        chosen, gain = ids[:, t:t + 1], gw[:, t:t + 1]
        high = high + jnp.where(lane == chosen, gain, 0.0)
        low = low + jnp.where(lane == chosen + ne, gain, 0.0)
    low = low - low.astype(jnp.bfloat16).astype(jnp.float32)
    zbuf[z, :, width:] = jnp.where(lane < ne, high, low).astype(jnp.bfloat16)
    pl.semaphore_wait(barrier, nz + ns - 1)

    def span(j):
        return pl.ds(j * cw, cw + (LANES if j == CHUNKS - 1 else 0))

    def a1(j, k):
        piece = zbuf.at[z, :, span(j)]
        return remote(piece, piece, a1_s.at[j, k - 1], a1_r.at[j, k - 1], (s, zpeer(k) * CORES + c))

    def source(k):
        return lax.rem(sy + ny - k // nx, ny) * nx + lax.rem(sx + nx - k % nx, nx)

    def xfirst(j):
        return j % 2 == 0

    def steps(j):
        ahead, beside = list(range(1, nx)), list(range(nx, ns, nx))
        return (ahead, beside) if xfirst(j) else (beside, ahead)

    def a2(j, k, d):
        piece = xs.at[c, source(k), :, span(j)]
        to = xpeer(d) if d < nx else ypeer(d // nx)
        return remote(piece, piece, a2_s.at[j, k + d - 1], a2_r.at[j, k + d - 1], to)

    def a2_wait(j, k):
        piece = xs.at[c, source(k), :, span(j)]
        remote(piece, piece, a2_s.at[j, k - 1], a2_r.at[j, k - 1], xpeer(1)).wait_recv()

    def a2_sent(j, k):
        piece = xs.at[c, source(k), :, span(j)]
        remote(piece, piece, a2_s.at[j, k - 1], a2_r.at[j, k - 1], xpeer(1)).wait_send()

    def a3(j, k):
        piece = xs.at[c, source(k), :, span(j)]
        return remote(piece, piece, a3_s.at[j, k], a3_r.at[j, k], sib)

    def cut(i, p):
        return pl.ds(pl.multiple_of((2 * i + p) * size, size), size)

    def share(k, i):
        cols = cut(i, plane)
        return remote(
            snap_hbm.at[c, :, cols], snap.at[sx, c, :, cols], sn_s.at[k - 1, i], sn_r.at[k - 1, i], xpeer(k)
        )

    def swap(k, i):
        piece = snap.at[xfrom(k), c, :, cut(i, plane)]
        return remote(piece, piece, sz_s.at[k - 1, i], sz_r.at[k - 1, i], other_plane)

    def forward(k, i, p):
        piece = snap.at[xfrom(k), c, :, cut(i, plane if p == 0 else 1 - plane)]
        return remote(piece, piece, sf_s.at[k - 1, i, p], sf_r.at[k - 1, i, p], sib)

    def ask(k):
        return (
            remote(q, qbuf.at[k - 1], q_s.at[k - 1, 0], q_r.at[k - 1, 0], ypeer(k)),
            remote(pick.at[0], pick.at[k], q_s.at[k - 1, 1], q_r.at[k - 1, 1], ypeer(k)),
        )

    def answer(k):
        back = ypeer(ny - k)
        return (
            remote(part_s.at[k - 1], part_r.at[k - 1], p_s.at[k - 1, 0], p_r.at[k - 1, 0], back),
            remote(stat_s.at[k - 1], stat_r.at[k - 1], p_s.at[k - 1, 1], p_r.at[k - 1, 1], back),
        )

    choice = lax.broadcasted_iota(jnp.int32, pick.shape[1:], 0)
    mine = jnp.zeros(pick.shape[1:], jnp.float32)
    for i in range(rows):
        mine = jnp.where(choice == i, leaf[i].astype(jnp.float32), mine)
    pick[0] = mine

    for j in range(CHUNKS):
        for k in range(1, nz):
            a1(j, k).start()

    for k in range(1, ny):
        for copy in ask(k):
            copy.start()
    for k in range(1, nx):
        for i in range(PIECES):
            share(k, i).start()

    own_f = own[...].astype(jnp.float32)
    for i in range(rows):
        part = pl.ds(i * heads, heads)
        own_score = qk_scale * jnp.sum(
            q[part, :].astype(jnp.float32) * own_f[i:i + 1], axis=1, keepdims=True
        )
        m_s[0, part, :] = jnp.broadcast_to(own_score, (heads, LANES))
        acc[0, part, :] = jnp.broadcast_to(own_f[i:i + 1, :LAT], (heads, LAT))
    l_s[0] = jnp.ones(l_s.shape[1:], jnp.float32)
    for k in range(1, ny):
        m_s[k] = jnp.full(m_s.shape[1:], -jnp.inf, jnp.float32)
        l_s[k] = jnp.zeros(l_s.shape[1:], jnp.float32)
        acc[k] = jnp.zeros(acc.shape[1:], jnp.float32)

    def attend(group, source):
        second = jnp.concatenate(
            [jnp.broadcast_to(pick[group, i:i + 1, :1], (heads, positions)) for i in range(rows)], axis=0
        ) > 0.5
        keys0, keys1 = snap[source, 0], snap[source, 1]
        queries = q[...] if group == 0 else qbuf[group - 1]
        score0 = jnp.dot(queries, keys0, preferred_element_type=jnp.float32)
        score1 = jnp.dot(queries, keys1, preferred_element_type=jnp.float32)
        score = qk_scale * jnp.where(second, score1, score0)
        before = m_s[group, :, :1]
        now = jnp.maximum(before, jnp.max(score, axis=1, keepdims=True))
        weight = jnp.exp(score - now).astype(jnp.bfloat16).astype(jnp.float32)
        decay = jnp.exp(before - now)
        l_s[group] = l_s[group] * decay + jnp.sum(weight, axis=1, keepdims=True)
        m_s[group] = jnp.broadcast_to(now, m_s.shape[1:])
        weight0 = jnp.where(second, 0.0, weight).astype(jnp.bfloat16)
        weight1 = jnp.where(second, weight, 0.0).astype(jnp.bfloat16)
        dims = (((1,), (1,)), ((), ()))
        acc[group] = (
            acc[group] * decay
            + lax.dot_general(weight0, keys0[:LAT], dims, preferred_element_type=jnp.float32)
            + lax.dot_general(weight1, keys1[:LAT], dims, preferred_element_type=jnp.float32)
        )

    own_copy.wait()
    attend(0, sx)

    for j in range(CHUNKS):
        for k in range(1, nz):
            a1(j, k).wait_recv()
        cols = span(j)
        for i in range(nz):
            asm[i * rows:(i + 1) * rows, cols] = zbuf[i, :, cols].astype(jnp.float32)
        xs[c, s, :, cols] = asm[:, cols].astype(jnp.bfloat16)
        first, second_step = steps(j)
        for d in first + second_step:
            a2(j, 0, d).start()
        a3(j, 0).start()

    for k in range(1, nx):
        for i in range(PIECES):
            share(k, i).wait_recv()
            swap(k, i).start()
            forward(k, i, 0).start()
    for j in range(CHUNKS):
        first, second_step = steps(j)
        for k in first:
            a2_wait(j, k)
            for d in second_step:
                a2(j, k, d).start()
            a3(j, k).start()
    for k in range(1, nx):
        for i in range(PIECES):
            swap(k, i).wait_recv()
            forward(k, i, 1).start()
    for k in range(1, ny):
        for copy in ask(k):
            copy.wait_recv()
        attend(k, sx)
    for k in range(1, nx):
        for i in range(PIECES):
            for p in range(2):
                forward(k, i, p).wait_recv()
    lane = lax.broadcasted_iota(jnp.int32, m_s.shape[1:], 1)
    for g in range(1, ny):
        def later(k, carry, g=g):
            attend(g, xfrom(k))
            return carry

        lax.fori_loop(1, nx, later, 0)
        part_s[g - 1] = acc[g].astype(jnp.bfloat16)
        stat_s[g - 1] = jnp.where(lane == 0, m_s[g], l_s[g]).T[:stat_s.shape[1]]
        for copy in answer(g):
            copy.start()

    total = CORES * ns * nz * rows

    def project(j, sums):
        for k in range(ns):
            a3(j, k).wait_recv()
        for copy in weight_copies[j]:
            copy.wait()
        part = pl.ds(j * cw, cw)
        block = xs[:, :, :, part].reshape(total, cw)
        gate_j = jnp.dot(block, wg_v[part, :], preferred_element_type=jnp.float32)
        up_j = jnp.dot(block, wu_v[part, :], preferred_element_type=jnp.float32)
        return (gate_j, up_j) if sums is None else (sums[0] + gate_j, sums[1] + up_j)

    sums = None
    for j in range(CHUNKS):
        first, _ = steps(j)
        for k in range(1, ns):
            if k not in first:
                a2_wait(j, k)
                a3(j, k).start()
        if j >= 1:
            sums = project(j - 1, sums)
    gate_proj, up_proj = project(CHUNKS - 1, sums)
    gains = xs[:, :, :, width:].reshape(total, LANES).astype(jnp.float32)
    lane = lax.broadcasted_iota(jnp.int32, (total, LANES), 1)
    gain = jnp.sum(jnp.where((lane == e) | (lane == e + ne), gains, 0.0), axis=1, keepdims=True)
    hid[...] = (gate_proj / (1.0 + jnp.exp(-gate_proj)) * up_proj * gain).astype(jnp.bfloat16)

    def back1(j):
        return remote(pbuf.at[j, 1 - c], r1.at[j], b1_s.at[j], b1_r.at[j], sib)

    def back2(j, k):
        return remote(
            r2s.at[j, speer(k)], r2r.at[j, k - 1], b2_s.at[j, k - 1], b2_r.at[j, k - 1], (speer(k), e)
        )

    def back3(j, k):
        return remote(
            r3s.at[j, zpeer(k)], r3r.at[j, k - 1], b3_s.at[j, k - 1], b3_r.at[j, k - 1],
            (s, zpeer(k) * CORES + c),
        )

    def spread(j):
        back1(j).wait_recv()
        r2s[j] = (pbuf[j, c].astype(jnp.float32) + r1[j].astype(jnp.float32)).astype(jnp.bfloat16)
        for k in range(1, ns):
            back2(j, k).start()

    for j in range(CHUNKS):
        down_copies[j].wait()
        partial = jnp.dot(hid[...], wd_v[:, pl.ds(j * cw, cw)], preferred_element_type=jnp.float32)
        pbuf[j] = partial.astype(jnp.bfloat16).reshape(pbuf.shape[1:])
        back1(j).start()
        if j >= 1:
            spread(j - 1)
    spread(CHUNKS - 1)

    def last(k, carry):
        attend(0, xfrom(k))
        return carry

    lax.fori_loop(1, nx, last, 0)
    top, mass, value = m_s[0, :, :1], l_s[0, :, :1], acc[0]
    for k in range(1, ny):
        for copy in answer(k):
            copy.wait_recv()
        blank = jnp.zeros((LANES - stat_r.shape[1], stat_r.shape[2]), jnp.float32)
        stats = jnp.concatenate([stat_r[k - 1], blank], axis=0).T
        other = stats[:, :1]
        now = jnp.maximum(top, other)
        mine, theirs = jnp.exp(top - now), jnp.exp(other - now)
        mass = mass * mine + stats[:, 1:2] * theirs
        value = value * mine + part_r[k - 1].astype(jnp.float32) * theirs
        top = now
    attn_out[...] = (value / mass).astype(attn_out.dtype)

    for j in range(CHUNKS):
        mine = r2s[j, s].astype(jnp.float32)
        for k in range(1, ns):
            back2(j, k).wait_recv()
            mine = mine + r2r[j, k - 1].astype(jnp.float32)
        asm[:, pl.ds(j * cw, cw)] = mine
        for i in range(nz):
            r3s[j, i] = asm[i * rows:(i + 1) * rows, pl.ds(j * cw, cw)].astype(jnp.bfloat16)
        for k in range(1, nz):
            back3(j, k).start()

    for j in range(CHUNKS):
        mine = r3s[j, z].astype(jnp.float32)
        for k in range(1, nz):
            back3(j, k).wait_recv()
            mine = mine + r3r[j, k - 1].astype(jnp.float32)
        moe_out[:, pl.ds(j * cw, cw)] = mine.astype(moe_out.dtype)

    for j in range(CHUNKS):
        for k in range(1, nz):
            a1(j, k).wait_send()
            back3(j, k).wait_send()
        for k in range(1, ns):
            a2_sent(j, k)
            back2(j, k).wait_send()
        for k in range(ns):
            a3(j, k).wait_send()
        back1(j).wait_send()
    for k in range(1, nx):
        for i in range(PIECES):
            share(k, i).wait_send()
            swap(k, i).wait_send()
            for p in range(2):
                forward(k, i, p).wait_send()
    for k in range(1, ny):
        for copy in ask(k) + answer(k):
            copy.wait_send()


def hand_out(attn, moe, attn_out, moe_out, sem):
    copies = [
        pltpu.make_async_copy(attn, attn_out, sem.at[0]),
        pltpu.make_async_copy(moe, moe_out, sem.at[1]),
    ]
    for copy in copies:
        copy.start()
    for copy in copies:
        copy.wait()


def body(
    queries, own_latent, snapshots, leaf_snapshot, moe_input, expert_ids, gate_weights,
    w_gate, w_up, w_down,
):
    ns, ne = lax.axis_size("seq"), lax.axis_size("exp")
    rows, heads, kdim = queries.shape
    width, ff = moe_input.shape[1], w_gate.shape[2]
    nz = ne // CORES
    group = nz * rows
    snaps, positions = snapshots.shape[:2]
    nx = math.isqrt(ns)
    ny = ns // nx
    assert nx * ny == ns and ny > 1
    lines = rows * heads
    cw = width // CHUNKS
    bf16, f32 = jnp.bfloat16, jnp.float32
    vmem = pl.BlockSpec(memory_space=pltpu.VMEM)
    smem = pl.BlockSpec(memory_space=pltpu.SMEM)
    hbm = pl.BlockSpec(memory_space=pl.ANY)
    dma = pltpu.SemaphoreType.DMA
    attn, moe = pl.pallas_call(
        functools.partial(kernel, ns, ne),
        out_shape=(
            jax.ShapeDtypeStruct((rows * heads, LAT), bf16),
            jax.ShapeDtypeStruct((rows, width), bf16),
        ),
        in_specs=[vmem, vmem, hbm, smem, vmem, vmem, vmem, hbm, hbm, hbm],
        out_specs=(vmem, vmem),
        scratch_shapes=[
            pltpu.VMEM((width, ff), bf16),
            pltpu.VMEM((width, ff), bf16),
            pltpu.VMEM((ff, width), bf16),
            pltpu.VMEM((nx, snaps, kdim, positions), bf16),
            pltpu.VMEM((nz, rows, width + LANES), bf16),
            pltpu.VMEM((group, width + LANES), f32),
            pltpu.VMEM((CORES, ns, group, width + LANES), bf16),
            pltpu.VMEM((CORES * ns * group, ff), bf16),
            pltpu.VMEM((CHUNKS, CORES, ns, group, cw), bf16),
            pltpu.VMEM((CHUNKS, ns, group, cw), bf16),
            pltpu.VMEM((CHUNKS, ns, group, cw), bf16),
            pltpu.VMEM((CHUNKS, ns - 1, group, cw), bf16),
            pltpu.VMEM((CHUNKS, nz, rows, cw), bf16),
            pltpu.VMEM((CHUNKS, nz - 1, rows, cw), bf16),
            pltpu.VMEM((ny, lines, LANES), f32),
            pltpu.VMEM((ny, lines, LANES), f32),
            pltpu.VMEM((ny, lines, LAT), f32),
            pltpu.VMEM((ny - 1, lines, kdim), bf16),
            pltpu.VMEM((ny, 8, LANES), f32),
            pltpu.VMEM((ny - 1, lines, LAT), bf16),
            pltpu.VMEM((ny - 1, lines, LAT), bf16),
            pltpu.VMEM((ny - 1, 8, lines), f32),
            pltpu.VMEM((ny - 1, 8, lines), f32),
            dma((3, CHUNKS)),
            dma,
            dma((CHUNKS, nz - 1)), dma((CHUNKS, nz - 1)),
            dma((CHUNKS, ns - 1)), dma((CHUNKS, ns - 1)),
            dma((CHUNKS, ns)), dma((CHUNKS, ns)),
            dma((nx - 1, PIECES)), dma((nx - 1, PIECES)),
            dma((nx - 1, PIECES)), dma((nx - 1, PIECES)),
            dma((nx - 1, PIECES, 2)), dma((nx - 1, PIECES, 2)),
            dma((CHUNKS,)), dma((CHUNKS,)),
            dma((CHUNKS, ns - 1)), dma((CHUNKS, ns - 1)),
            dma((CHUNKS, nz - 1)), dma((CHUNKS, nz - 1)),
            dma((ny - 1, 2)), dma((ny - 1, 2)),
            dma((ny - 1, 2)), dma((ny - 1, 2)),
        ],
        compiler_params=pltpu.CompilerParams(
            collective_id=0, has_side_effects=True, vmem_limit_bytes=62 * 1024 * 1024
        ),
    )(
        queries.reshape(rows * heads, kdim), own_latent, jnp.swapaxes(snapshots, 1, 2), leaf_snapshot,
        moe_input, expert_ids, gate_weights, w_gate, w_up, w_down,
    )
    attn, moe = pl.pallas_call(
        hand_out,
        out_shape=(jax.ShapeDtypeStruct(attn.shape, bf16), jax.ShapeDtypeStruct(moe.shape, bf16)),
        in_specs=[pl.BlockSpec(memory_space=pltpu.HBM)] * 2,
        out_specs=(pl.BlockSpec(memory_space=pltpu.HBM),) * 2,
        scratch_shapes=[dma((2,))],
    )(attn, moe)
    return attn.reshape(rows, heads, LAT), moe


def solution(mesh):
    in_specs = (
        P(("seq", "exp"), None, None),
        P(("seq", "exp"), None),
        P(None, "seq", None),
        P(("seq", "exp")),
        P(("seq", "exp"), None),
        P(("seq", "exp"), None),
        P(("seq", "exp"), None),
        P("exp", None, "seq"),
        P("exp", None, "seq"),
        P("exp", "seq", None),
    )
    out_specs = (P(("seq", "exp"), None, None), P(("seq", "exp"), None))
    return jax.shard_map(body, mesh=mesh, in_specs=in_specs, out_specs=out_specs, check_vma=False)
```

```python
import functools
import math

import jax
import jax.numpy as jnp
from jax import lax
from jax.experimental import pallas as pl
from jax.experimental.pallas import tpu as pltpu
from jax.sharding import PartitionSpec as P

LAT = 512
LANES = 128
CHUNKS = 4
CORES = 2
PIECES = 2
MESH = pl.DeviceIdType.MESH

qk_scale = 192.0 ** (-0.5)


def kernel(
    ns, ne, q_hbm, own, snap_hbm, leaf, x, ids, gw, wg, wu, wd, attn_hbm, moe_out,
    wg_v, wu_v, wd_v, snap, zbuf, asm, xs, hid, pbuf, r1, r2s, r2r, r3s, r3r, m_s, l_s, acc,
    q, attn_out, qbuf, pick, part_s, part_r, stat_s, stat_r,
    w_sem, sl_sem, io_sem, a1_s, a1_r, a2_s, a2_r, a3_s, a3_r, sn_s, sn_r, sz_s, sz_r, sf_s, sf_r,
    b1_s, b1_r, b2_s, b2_r, b3_s, b3_r, q_s, q_r, p_s, p_r,
):
    rows, width = x.shape
    nz = ne // CORES
    heads = q.shape[0] // rows
    cw = width // CHUNKS
    s, e = lax.axis_index("seq"), lax.axis_index("exp")
    z, c = e // CORES, e % CORES
    sib = (s, z * CORES + (1 - c))
    nx = math.isqrt(ns)
    ny = ns // nx
    sy, sx = s // nx, s % nx
    positions = snap.shape[3]
    size = positions // (2 * PIECES)
    plane = z % 2
    other_plane = (s, (z + 1 - 2 * plane) * CORES + c)

    def zpeer(k):
        return lax.rem(z + k, nz)

    def speer(k):
        return lax.rem(s + k, ns)

    def xpeer(k):
        return (sy * nx + lax.rem(sx + k, nx), e)

    def xfrom(k):
        return lax.rem(sx + nx - k, nx)

    def ypeer(k):
        return (lax.rem(sy + k, ny) * nx + sx, e)

    def yfrom(k):
        return lax.rem(sy + ny - k, ny)

    def remote(src, dst, send, recv, device):
        return pltpu.make_async_remote_copy(
            src_ref=src, dst_ref=dst, send_sem=send, recv_sem=recv,
            device_id=device, device_id_type=MESH,
        )

    q_copy = pltpu.make_async_copy(q_hbm, q, io_sem.at[0])
    q_copy.start()
    own_copy = pltpu.make_async_copy(snap_hbm, snap.at[sx], sl_sem)
    own_copy.start()
    weight_copies = []
    for j in range(CHUNKS):
        part = pl.ds(j * cw, cw)
        pair = [
            pltpu.make_async_copy(wg.at[0, part], wg_v.at[part], w_sem.at[0, j]),
            pltpu.make_async_copy(wu.at[0, part], wu_v.at[part], w_sem.at[1, j]),
        ]
        weight_copies.append(pair)
        for copy in pair:
            copy.start()
    down_copies = []
    for j in range(CHUNKS):
        part = pl.ds(j * cw, cw)
        copy = pltpu.make_async_copy(wd.at[0, :, part], wd_v.at[:, part], w_sem.at[2, j])
        copy.start()
        down_copies.append(copy)

    barrier = pltpu.get_barrier_semaphore()
    for k in range(1, nz):
        pl.semaphore_signal(barrier, inc=1, device_id=(s, zpeer(k) * CORES + c), device_id_type=MESH)
    for k in range(1, ns):
        pl.semaphore_signal(barrier, inc=1, device_id=(speer(k), e), device_id_type=MESH)
    pl.semaphore_signal(barrier, inc=1, device_id=sib, device_id_type=MESH)

    zbuf[z, :, :width] = x[...]
    lane = lax.broadcasted_iota(jnp.int32, (rows, LANES), 1)
    high = jnp.zeros((rows, LANES), jnp.float32)
    low = jnp.zeros((rows, LANES), jnp.float32)
    for t in range(ids.shape[1]):
        chosen, gain = ids[:, t:t + 1], gw[:, t:t + 1]
        high = high + jnp.where(lane == chosen, gain, 0.0)
        low = low + jnp.where(lane == chosen + ne, gain, 0.0)
    low = low - low.astype(jnp.bfloat16).astype(jnp.float32)
    zbuf[z, :, width:] = jnp.where(lane < ne, high, low).astype(jnp.bfloat16)
    pl.semaphore_wait(barrier, nz + ns - 1)

    def span(j):
        return pl.ds(j * cw, cw + (LANES if j == CHUNKS - 1 else 0))

    def a1(j, k):
        piece = zbuf.at[z, :, span(j)]
        return remote(piece, piece, a1_s.at[j, k - 1], a1_r.at[j, k - 1], (s, zpeer(k) * CORES + c))

    def source(k):
        return lax.rem(sy + ny - k // nx, ny) * nx + lax.rem(sx + nx - k % nx, nx)

    def xfirst(j):
        return j % 2 == 0

    def steps(j):
        ahead, beside = list(range(1, nx)), list(range(nx, ns, nx))
        return (ahead, beside) if xfirst(j) else (beside, ahead)

    def a2(j, k, d):
        piece = xs.at[c, source(k), :, span(j)]
        to = xpeer(d) if d < nx else ypeer(d // nx)
        return remote(piece, piece, a2_s.at[j, k + d - 1], a2_r.at[j, k + d - 1], to)

    def a2_wait(j, k):
        piece = xs.at[c, source(k), :, span(j)]
        remote(piece, piece, a2_s.at[j, k - 1], a2_r.at[j, k - 1], xpeer(1)).wait_recv()

    def a2_sent(j, k):
        piece = xs.at[c, source(k), :, span(j)]
        remote(piece, piece, a2_s.at[j, k - 1], a2_r.at[j, k - 1], xpeer(1)).wait_send()

    def a3(j, k):
        piece = xs.at[c, source(k), :, span(j)]
        return remote(piece, piece, a3_s.at[j, k], a3_r.at[j, k], sib)

    def cut(i, p):
        return pl.ds(pl.multiple_of((2 * i + p) * size, size), size)

    def share(k, i):
        cols = cut(i, plane)
        return remote(
            snap_hbm.at[c, :, cols], snap.at[sx, c, :, cols], sn_s.at[k - 1, i], sn_r.at[k - 1, i], xpeer(k)
        )

    def swap(k, i):
        piece = snap.at[xfrom(k), c, :, cut(i, plane)]
        return remote(piece, piece, sz_s.at[k - 1, i], sz_r.at[k - 1, i], other_plane)

    def forward(k, i, p):
        piece = snap.at[xfrom(k), c, :, cut(i, plane if p == 0 else 1 - plane)]
        return remote(piece, piece, sf_s.at[k - 1, i, p], sf_r.at[k - 1, i, p], sib)

    def ask(k):
        return (
            remote(q_hbm, qbuf.at[k - 1], q_s.at[k - 1, 0], q_r.at[k - 1, 0], ypeer(k)),
            remote(pick.at[0], pick.at[k], q_s.at[k - 1, 1], q_r.at[k - 1, 1], ypeer(k)),
        )

    def answer(k):
        back = ypeer(ny - k)
        return (
            remote(part_s.at[k - 1], part_r.at[k - 1], p_s.at[k - 1, 0], p_r.at[k - 1, 0], back),
            remote(stat_s.at[k - 1], stat_r.at[k - 1], p_s.at[k - 1, 1], p_r.at[k - 1, 1], back),
        )

    choice = lax.broadcasted_iota(jnp.int32, pick.shape[1:], 0)
    mine = jnp.zeros(pick.shape[1:], jnp.float32)
    for i in range(rows):
        mine = jnp.where(choice == i, leaf[i].astype(jnp.float32), mine)
    pick[0] = mine

    for j in range(CHUNKS):
        for k in range(1, nz):
            a1(j, k).start()

    for k in range(1, ny):
        for copy in ask(k):
            copy.start()
    for k in range(1, nx):
        for i in range(PIECES):
            share(k, i).start()

    q_copy.wait()
    own_f = own[...].astype(jnp.float32)
    for i in range(rows):
        part = pl.ds(i * heads, heads)
        own_score = qk_scale * jnp.sum(
            q[part, :].astype(jnp.float32) * own_f[i:i + 1], axis=1, keepdims=True
        )
        m_s[0, part, :] = jnp.broadcast_to(own_score, (heads, LANES))
        acc[0, part, :] = jnp.broadcast_to(own_f[i:i + 1, :LAT], (heads, LAT))
    l_s[0] = jnp.ones(l_s.shape[1:], jnp.float32)
    for k in range(1, ny):
        m_s[k] = jnp.full(m_s.shape[1:], -jnp.inf, jnp.float32)
        l_s[k] = jnp.zeros(l_s.shape[1:], jnp.float32)
        acc[k] = jnp.zeros(acc.shape[1:], jnp.float32)

    def attend(group, source):
        second = jnp.concatenate(
            [jnp.broadcast_to(pick[group, i:i + 1, :1], (heads, positions)) for i in range(rows)], axis=0
        ) > 0.5
        keys0, keys1 = snap[source, 0], snap[source, 1]
        queries = q[...] if group == 0 else qbuf[group - 1]
        score0 = jnp.dot(queries, keys0, preferred_element_type=jnp.float32)
        score1 = jnp.dot(queries, keys1, preferred_element_type=jnp.float32)
        score = qk_scale * jnp.where(second, score1, score0)
        before = m_s[group, :, :1]
        now = jnp.maximum(before, jnp.max(score, axis=1, keepdims=True))
        weight = jnp.exp(score - now).astype(jnp.bfloat16).astype(jnp.float32)
        decay = jnp.exp(before - now)
        l_s[group] = l_s[group] * decay + jnp.sum(weight, axis=1, keepdims=True)
        m_s[group] = jnp.broadcast_to(now, m_s.shape[1:])
        weight0 = jnp.where(second, 0.0, weight).astype(jnp.bfloat16)
        weight1 = jnp.where(second, weight, 0.0).astype(jnp.bfloat16)
        dims = (((1,), (1,)), ((), ()))
        acc[group] = (
            acc[group] * decay
            + lax.dot_general(weight0, keys0[:LAT], dims, preferred_element_type=jnp.float32)
            + lax.dot_general(weight1, keys1[:LAT], dims, preferred_element_type=jnp.float32)
        )

    own_copy.wait()
    attend(0, sx)

    for j in range(CHUNKS):
        for k in range(1, nz):
            a1(j, k).wait_recv()
        cols = span(j)
        for i in range(nz):
            asm[i * rows:(i + 1) * rows, cols] = zbuf[i, :, cols].astype(jnp.float32)
        xs[c, s, :, cols] = asm[:, cols].astype(jnp.bfloat16)
        first, second_step = steps(j)
        for d in first + second_step:
            a2(j, 0, d).start()
        a3(j, 0).start()

    for k in range(1, nx):
        for i in range(PIECES):
            share(k, i).wait_recv()
            swap(k, i).start()
            forward(k, i, 0).start()
    for j in range(CHUNKS):
        first, second_step = steps(j)
        for k in first:
            a2_wait(j, k)
            for d in second_step:
                a2(j, k, d).start()
            a3(j, k).start()
    for k in range(1, nx):
        for i in range(PIECES):
            swap(k, i).wait_recv()
            forward(k, i, 1).start()
    for k in range(1, ny):
        for copy in ask(k):
            copy.wait_recv()
        attend(k, sx)

    def pass_on(j):
        first, _ = steps(j)
        for k in range(1, ns):
            if k not in first:
                a2_wait(j, k)
                a3(j, k).start()

    for j in range(CHUNKS // 2):
        pass_on(j)
    for k in range(1, nx):
        for i in range(PIECES):
            for p in range(2):
                forward(k, i, p).wait_recv()
    lane = lax.broadcasted_iota(jnp.int32, m_s.shape[1:], 1)
    for g in range(1, ny):
        def later(k, carry, g=g):
            attend(g, xfrom(k))
            return carry

        lax.fori_loop(1, nx, later, 0)
        part_s[g - 1] = acc[g].astype(jnp.bfloat16)
        stat_s[g - 1] = jnp.where(lane == 0, m_s[g], l_s[g]).T[:stat_s.shape[1]]
        for copy in answer(g):
            copy.start()

    total = CORES * ns * nz * rows

    def project(j, sums):
        for k in range(ns):
            a3(j, k).wait_recv()
        for copy in weight_copies[j]:
            copy.wait()
        part = pl.ds(j * cw, cw)
        block = xs[:, :, :, part].reshape(total, cw)
        gate_j = jnp.dot(block, wg_v[part, :], preferred_element_type=jnp.float32)
        up_j = jnp.dot(block, wu_v[part, :], preferred_element_type=jnp.float32)
        return (gate_j, up_j) if sums is None else (sums[0] + gate_j, sums[1] + up_j)

    sums = None
    for j in range(CHUNKS):
        if j >= CHUNKS // 2:
            pass_on(j)
        if j >= 1:
            sums = project(j - 1, sums)
    gate_proj, up_proj = project(CHUNKS - 1, sums)
    gains = xs[:, :, :, width:].reshape(total, LANES).astype(jnp.float32)
    lane = lax.broadcasted_iota(jnp.int32, (total, LANES), 1)
    gain = jnp.sum(jnp.where((lane == e) | (lane == e + ne), gains, 0.0), axis=1, keepdims=True)
    hid[...] = (gate_proj / (1.0 + jnp.exp(-gate_proj)) * up_proj * gain).astype(jnp.bfloat16)

    def back1(j):
        return remote(pbuf.at[j, 1 - c], r1.at[j], b1_s.at[j], b1_r.at[j], sib)

    def back2(j, k):
        return remote(
            r2s.at[j, speer(k)], r2r.at[j, k - 1], b2_s.at[j, k - 1], b2_r.at[j, k - 1], (speer(k), e)
        )

    def back3(j, k):
        return remote(
            r3s.at[j, zpeer(k)], r3r.at[j, k - 1], b3_s.at[j, k - 1], b3_r.at[j, k - 1],
            (s, zpeer(k) * CORES + c),
        )

    def spread(j):
        back1(j).wait_recv()
        r2s[j] = (pbuf[j, c].astype(jnp.float32) + r1[j].astype(jnp.float32)).astype(jnp.bfloat16)
        for k in range(1, ns):
            back2(j, k).start()

    for j in range(CHUNKS):
        down_copies[j].wait()
        partial = jnp.dot(hid[...], wd_v[:, pl.ds(j * cw, cw)], preferred_element_type=jnp.float32)
        pbuf[j] = partial.astype(jnp.bfloat16).reshape(pbuf.shape[1:])
        back1(j).start()
        if j >= 1:
            spread(j - 1)
    spread(CHUNKS - 1)

    def last(k, carry):
        attend(0, xfrom(k))
        return carry

    lax.fori_loop(1, nx, last, 0)
    top, mass, value = m_s[0, :, :1], l_s[0, :, :1], acc[0]
    for k in range(1, ny):
        for copy in answer(k):
            copy.wait_recv()
        blank = jnp.zeros((LANES - stat_r.shape[1], stat_r.shape[2]), jnp.float32)
        stats = jnp.concatenate([stat_r[k - 1], blank], axis=0).T
        other = stats[:, :1]
        now = jnp.maximum(top, other)
        mine, theirs = jnp.exp(top - now), jnp.exp(other - now)
        mass = mass * mine + stats[:, 1:2] * theirs
        value = value * mine + part_r[k - 1].astype(jnp.float32) * theirs
        top = now
    attn_out[...] = (value / mass).astype(attn_out.dtype)
    attn_copy = pltpu.make_async_copy(attn_out, attn_hbm, io_sem.at[1])
    attn_copy.start()

    for j in range(CHUNKS):
        mine = r2s[j, s].astype(jnp.float32)
        for k in range(1, ns):
            back2(j, k).wait_recv()
            mine = mine + r2r[j, k - 1].astype(jnp.float32)
        asm[:, pl.ds(j * cw, cw)] = mine
        for i in range(nz):
            r3s[j, i] = asm[i * rows:(i + 1) * rows, pl.ds(j * cw, cw)].astype(jnp.bfloat16)
        for k in range(1, nz):
            back3(j, k).start()

    for j in range(CHUNKS):
        mine = r3s[j, z].astype(jnp.float32)
        for k in range(1, nz):
            back3(j, k).wait_recv()
            mine = mine + r3r[j, k - 1].astype(jnp.float32)
        moe_out[:, pl.ds(j * cw, cw)] = mine.astype(moe_out.dtype)

    for j in range(CHUNKS):
        for k in range(1, nz):
            a1(j, k).wait_send()
            back3(j, k).wait_send()
        for k in range(1, ns):
            a2_sent(j, k)
            back2(j, k).wait_send()
        for k in range(ns):
            a3(j, k).wait_send()
        back1(j).wait_send()
    for k in range(1, nx):
        for i in range(PIECES):
            share(k, i).wait_send()
            swap(k, i).wait_send()
            for p in range(2):
                forward(k, i, p).wait_send()
    attn_copy.wait()
    for k in range(1, ny):
        for copy in ask(k) + answer(k):
            copy.wait_send()


def hand_out(attn, moe, attn_out, moe_out):
    attn_out[...] = attn[...]
    moe_out[...] = moe[...]


def body(
    queries, own_latent, snapshots, leaf_snapshot, moe_input, expert_ids, gate_weights,
    w_gate, w_up, w_down,
):
    ns, ne = lax.axis_size("seq"), lax.axis_size("exp")
    rows, heads, kdim = queries.shape
    width, ff = moe_input.shape[1], w_gate.shape[2]
    nz = ne // CORES
    group = nz * rows
    snaps, positions = snapshots.shape[:2]
    nx = math.isqrt(ns)
    ny = ns // nx
    assert nx * ny == ns and ny > 1
    lines = rows * heads
    cw = width // CHUNKS
    bf16, f32 = jnp.bfloat16, jnp.float32
    vmem = pl.BlockSpec(memory_space=pltpu.VMEM)
    smem = pl.BlockSpec(memory_space=pltpu.SMEM)
    hbm = pl.BlockSpec(memory_space=pl.ANY)
    dma = pltpu.SemaphoreType.DMA
    attn, moe = pl.pallas_call(
        functools.partial(kernel, ns, ne),
        out_shape=(
            jax.ShapeDtypeStruct((rows * heads, LAT), bf16),
            jax.ShapeDtypeStruct((rows, width), bf16),
        ),
        in_specs=[hbm, vmem, hbm, smem, vmem, vmem, vmem, hbm, hbm, hbm],
        out_specs=(hbm, vmem),
        scratch_shapes=[
            pltpu.VMEM((width, ff), bf16),
            pltpu.VMEM((width, ff), bf16),
            pltpu.VMEM((ff, width), bf16),
            pltpu.VMEM((nx, snaps, kdim, positions), bf16),
            pltpu.VMEM((nz, rows, width + LANES), bf16),
            pltpu.VMEM((group, width + LANES), f32),
            pltpu.VMEM((CORES, ns, group, width + LANES), bf16),
            pltpu.VMEM((CORES * ns * group, ff), bf16),
            pltpu.VMEM((CHUNKS, CORES, ns, group, cw), bf16),
            pltpu.VMEM((CHUNKS, ns, group, cw), bf16),
            pltpu.VMEM((CHUNKS, ns, group, cw), bf16),
            pltpu.VMEM((CHUNKS, ns - 1, group, cw), bf16),
            pltpu.VMEM((CHUNKS, nz, rows, cw), bf16),
            pltpu.VMEM((CHUNKS, nz - 1, rows, cw), bf16),
            pltpu.VMEM((ny, lines, LANES), f32),
            pltpu.VMEM((ny, lines, LANES), f32),
            pltpu.VMEM((ny, lines, LAT), f32),
            pltpu.VMEM((lines, kdim), bf16),
            pltpu.VMEM((lines, LAT), bf16),
            pltpu.VMEM((ny - 1, lines, kdim), bf16),
            pltpu.VMEM((ny, 8, LANES), f32),
            pltpu.VMEM((ny - 1, lines, LAT), bf16),
            pltpu.VMEM((ny - 1, lines, LAT), bf16),
            pltpu.VMEM((ny - 1, 8, lines), f32),
            pltpu.VMEM((ny - 1, 8, lines), f32),
            dma((3, CHUNKS)),
            dma,
            dma((2,)),
            dma((CHUNKS, nz - 1)), dma((CHUNKS, nz - 1)),
            dma((CHUNKS, ns - 1)), dma((CHUNKS, ns - 1)),
            dma((CHUNKS, ns)), dma((CHUNKS, ns)),
            dma((nx - 1, PIECES)), dma((nx - 1, PIECES)),
            dma((nx - 1, PIECES)), dma((nx - 1, PIECES)),
            dma((nx - 1, PIECES, 2)), dma((nx - 1, PIECES, 2)),
            dma((CHUNKS,)), dma((CHUNKS,)),
            dma((CHUNKS, ns - 1)), dma((CHUNKS, ns - 1)),
            dma((CHUNKS, nz - 1)), dma((CHUNKS, nz - 1)),
            dma((ny - 1, 2)), dma((ny - 1, 2)),
            dma((ny - 1, 2)), dma((ny - 1, 2)),
        ],
        compiler_params=pltpu.CompilerParams(
            collective_id=0, has_side_effects=True, vmem_limit_bytes=62 * 1024 * 1024
        ),
    )(
        queries.reshape(rows * heads, kdim), own_latent, jnp.swapaxes(snapshots, 1, 2), leaf_snapshot,
        moe_input, expert_ids, gate_weights, w_gate, w_up, w_down,
    )
    attn, moe = pl.pallas_call(
        hand_out,
        out_shape=(jax.ShapeDtypeStruct(attn.shape, bf16), jax.ShapeDtypeStruct(moe.shape, bf16)),
        in_specs=[vmem, vmem],
        out_specs=(vmem, vmem),
    )(attn, moe)
    return attn.reshape(rows, heads, LAT), moe


def solution(mesh):
    in_specs = (
        P(("seq", "exp"), None, None),
        P(("seq", "exp"), None),
        P(None, "seq", None),
        P(("seq", "exp")),
        P(("seq", "exp"), None),
        P(("seq", "exp"), None),
        P(("seq", "exp"), None),
        P("exp", None, "seq"),
        P("exp", None, "seq"),
        P("exp", "seq", None),
    )
    out_specs = (P(("seq", "exp"), None, None), P(("seq", "exp"), None))
    return jax.shard_map(body, mesh=mesh, in_specs=in_specs, out_specs=out_specs, check_vma=False)
```

```python
import functools
import math

import jax
import jax.numpy as jnp
from jax import lax
from jax.experimental import pallas as pl
from jax.experimental.pallas import tpu as pltpu
from jax.sharding import PartitionSpec as P

LAT = 512
LANES = 128
CHUNKS = 4
CORES = 2
PIECES = 2
MESH = pl.DeviceIdType.MESH

qk_scale = 192.0 ** (-0.5)


def kernel(
    ns, ne, q_hbm, own, snap_hbm, leaf, x, ids, gw, wg, wu, wd, attn_hbm, moe_out,
    wg_v, wu_v, wd_v, snap, zbuf, asm, xs, hid, pbuf, r1, r2s, r2r, r3s, r3r, m_s, l_s, acc,
    q, attn_out, qbuf, pick, part_s, part_r, stat_s, stat_r,
    w_sem, sl_sem, io_sem, a1_s, a1_r, a2_s, a2_r, a3_s, a3_r, sn_s, sn_r, sz_s, sz_r, sf_s, sf_r,
    b1_s, b1_r, b2_s, b2_r, b3_s, b3_r, q_s, q_r, p_s, p_r,
):
    rows, width = x.shape
    nz = ne // CORES
    heads = q.shape[0] // rows
    cw = width // CHUNKS
    s, e = lax.axis_index("seq"), lax.axis_index("exp")
    z, c = e // CORES, e % CORES
    sib = (s, z * CORES + (1 - c))
    nx = math.isqrt(ns)
    ny = ns // nx
    sy, sx = s // nx, s % nx
    positions = snap.shape[3]
    size = positions // (2 * PIECES)
    plane = z % 2
    other_plane = (s, (z + 1 - 2 * plane) * CORES + c)

    def zpeer(k):
        return lax.rem(z + k, nz)

    def speer(k):
        return lax.rem(s + k, ns)

    def xpeer(k):
        return (sy * nx + lax.rem(sx + k, nx), e)

    def xfrom(k):
        return lax.rem(sx + nx - k, nx)

    def ypeer(k):
        return (lax.rem(sy + k, ny) * nx + sx, e)

    def yfrom(k):
        return lax.rem(sy + ny - k, ny)

    def remote(src, dst, send, recv, device):
        return pltpu.make_async_remote_copy(
            src_ref=src, dst_ref=dst, send_sem=send, recv_sem=recv,
            device_id=device, device_id_type=MESH,
        )

    q_copy = pltpu.make_async_copy(q_hbm, q, io_sem.at[0])
    q_copy.start()
    own_copy = pltpu.make_async_copy(snap_hbm, snap.at[sx], sl_sem)
    own_copy.start()
    weight_copies = []
    for j in range(CHUNKS):
        part = pl.ds(j * cw, cw)
        pair = [
            pltpu.make_async_copy(wg.at[0, part], wg_v.at[part], w_sem.at[0, j]),
            pltpu.make_async_copy(wu.at[0, part], wu_v.at[part], w_sem.at[1, j]),
        ]
        weight_copies.append(pair)
        for copy in pair:
            copy.start()
    down_copies = []
    for j in range(CHUNKS):
        part = pl.ds(j * cw, cw)
        copy = pltpu.make_async_copy(wd.at[0, :, part], wd_v.at[:, part], w_sem.at[2, j])
        copy.start()
        down_copies.append(copy)

    barrier = pltpu.get_barrier_semaphore()
    for k in range(1, nz):
        pl.semaphore_signal(barrier, inc=1, device_id=(s, zpeer(k) * CORES + c), device_id_type=MESH)
    for k in range(1, ns):
        pl.semaphore_signal(barrier, inc=1, device_id=(speer(k), e), device_id_type=MESH)
    pl.semaphore_signal(barrier, inc=1, device_id=sib, device_id_type=MESH)

    zbuf[z, :, :width] = x[...]
    lane = lax.broadcasted_iota(jnp.int32, (rows, LANES), 1)
    high = jnp.zeros((rows, LANES), jnp.float32)
    low = jnp.zeros((rows, LANES), jnp.float32)
    for t in range(ids.shape[1]):
        chosen, gain = ids[:, t:t + 1], gw[:, t:t + 1]
        high = high + jnp.where(lane == chosen, gain, 0.0)
        low = low + jnp.where(lane == chosen + ne, gain, 0.0)
    low = low - low.astype(jnp.bfloat16).astype(jnp.float32)
    zbuf[z, :, width:] = jnp.where(lane < ne, high, low).astype(jnp.bfloat16)
    pl.semaphore_wait(barrier, nz + ns - 1)

    def span(j):
        return pl.ds(j * cw, cw + (LANES if j == CHUNKS - 1 else 0))

    def a1(j, k):
        piece = zbuf.at[z, :, span(j)]
        return remote(piece, piece, a1_s.at[j, k - 1], a1_r.at[j, k - 1], (s, zpeer(k) * CORES + c))

    def source(k):
        return lax.rem(sy + ny - k // nx, ny) * nx + lax.rem(sx + nx - k % nx, nx)

    def steps(j):
        return list(range(nx, ns, nx)), list(range(1, nx))

    def a2(j, k, d):
        piece = xs.at[c, source(k), :, span(j)]
        to = xpeer(d) if d < nx else ypeer(d // nx)
        return remote(piece, piece, a2_s.at[j, k + d - 1], a2_r.at[j, k + d - 1], to)

    def a2_wait(j, k):
        piece = xs.at[c, source(k), :, span(j)]
        remote(piece, piece, a2_s.at[j, k - 1], a2_r.at[j, k - 1], xpeer(1)).wait_recv()

    def a2_sent(j, k):
        piece = xs.at[c, source(k), :, span(j)]
        remote(piece, piece, a2_s.at[j, k - 1], a2_r.at[j, k - 1], xpeer(1)).wait_send()

    def a3(j, k):
        piece = xs.at[c, source(k), :, span(j)]
        return remote(piece, piece, a3_s.at[j, k], a3_r.at[j, k], sib)

    def cut(i, p):
        return pl.ds(pl.multiple_of((2 * i + p) * size, size), size)

    def share(k, i):
        cols = cut(i, plane)
        return remote(
            snap_hbm.at[c, :, cols], snap.at[sx, c, :, cols], sn_s.at[k - 1, i], sn_r.at[k - 1, i], xpeer(k)
        )

    def swap(k, i):
        piece = snap.at[xfrom(k), c, :, cut(i, plane)]
        return remote(piece, piece, sz_s.at[k - 1, i], sz_r.at[k - 1, i], other_plane)

    def forward(k, i, p):
        piece = snap.at[xfrom(k), c, :, cut(i, plane if p == 0 else 1 - plane)]
        return remote(piece, piece, sf_s.at[k - 1, i, p], sf_r.at[k - 1, i, p], sib)

    def ask(k):
        return (
            remote(q_hbm, qbuf.at[k - 1], q_s.at[k - 1, 0], q_r.at[k - 1, 0], ypeer(k)),
            remote(pick.at[0], pick.at[k], q_s.at[k - 1, 1], q_r.at[k - 1, 1], ypeer(k)),
        )

    def answer(k):
        back = ypeer(ny - k)
        return (
            remote(part_s.at[k - 1], part_r.at[k - 1], p_s.at[k - 1, 0], p_r.at[k - 1, 0], back),
            remote(stat_s.at[k - 1], stat_r.at[k - 1], p_s.at[k - 1, 1], p_r.at[k - 1, 1], back),
        )

    choice = lax.broadcasted_iota(jnp.int32, pick.shape[1:], 0)
    mine = jnp.zeros(pick.shape[1:], jnp.float32)
    for i in range(rows):
        mine = jnp.where(choice == i, leaf[i].astype(jnp.float32), mine)
    pick[0] = mine

    for j in range(CHUNKS):
        for k in range(1, nz):
            a1(j, k).start()

    for k in range(1, ny):
        for copy in ask(k):
            copy.start()
    for k in range(1, nx):
        for i in range(PIECES):
            share(k, i).start()

    q_copy.wait()
    own_f = own[...].astype(jnp.float32)
    for i in range(rows):
        part = pl.ds(i * heads, heads)
        own_score = qk_scale * jnp.sum(
            q[part, :].astype(jnp.float32) * own_f[i:i + 1], axis=1, keepdims=True
        )
        m_s[0, part, :] = jnp.broadcast_to(own_score, (heads, LANES))
        acc[0, part, :] = jnp.broadcast_to(own_f[i:i + 1, :LAT], (heads, LAT))
    l_s[0] = jnp.ones(l_s.shape[1:], jnp.float32)
    for k in range(1, ny):
        m_s[k] = jnp.full(m_s.shape[1:], -jnp.inf, jnp.float32)
        l_s[k] = jnp.zeros(l_s.shape[1:], jnp.float32)
        acc[k] = jnp.zeros(acc.shape[1:], jnp.float32)

    def attend(group, source):
        second = jnp.concatenate(
            [jnp.broadcast_to(pick[group, i:i + 1, :1], (heads, positions)) for i in range(rows)], axis=0
        ) > 0.5
        keys0, keys1 = snap[source, 0], snap[source, 1]
        queries = q[...] if group == 0 else qbuf[group - 1]
        score0 = jnp.dot(queries, keys0, preferred_element_type=jnp.float32)
        score1 = jnp.dot(queries, keys1, preferred_element_type=jnp.float32)
        score = qk_scale * jnp.where(second, score1, score0)
        before = m_s[group, :, :1]
        now = jnp.maximum(before, jnp.max(score, axis=1, keepdims=True))
        weight = jnp.exp(score - now).astype(jnp.bfloat16).astype(jnp.float32)
        decay = jnp.exp(before - now)
        l_s[group] = l_s[group] * decay + jnp.sum(weight, axis=1, keepdims=True)
        m_s[group] = jnp.broadcast_to(now, m_s.shape[1:])
        weight0 = jnp.where(second, 0.0, weight).astype(jnp.bfloat16)
        weight1 = jnp.where(second, weight, 0.0).astype(jnp.bfloat16)
        dims = (((1,), (1,)), ((), ()))
        acc[group] = (
            acc[group] * decay
            + lax.dot_general(weight0, keys0[:LAT], dims, preferred_element_type=jnp.float32)
            + lax.dot_general(weight1, keys1[:LAT], dims, preferred_element_type=jnp.float32)
        )

    own_copy.wait()
    attend(0, sx)

    for j in range(CHUNKS):
        for k in range(1, nz):
            a1(j, k).wait_recv()
        cols = span(j)
        for i in range(nz):
            asm[i * rows:(i + 1) * rows, cols] = zbuf[i, :, cols].astype(jnp.float32)
        xs[c, s, :, cols] = asm[:, cols].astype(jnp.bfloat16)
        first, second_step = steps(j)
        for d in first + second_step:
            a2(j, 0, d).start()
        a3(j, 0).start()

    for k in range(1, nx):
        for i in range(PIECES):
            share(k, i).wait_recv()
            swap(k, i).start()
            forward(k, i, 0).start()
    for j in range(CHUNKS):
        first, second_step = steps(j)
        for k in first:
            a2_wait(j, k)
            for d in second_step:
                a2(j, k, d).start()
            a3(j, k).start()
    for k in range(1, nx):
        for i in range(PIECES):
            swap(k, i).wait_recv()
            forward(k, i, 1).start()
    for k in range(1, ny):
        for copy in ask(k):
            copy.wait_recv()
        attend(k, sx)

    def pass_on(j):
        first, _ = steps(j)
        for k in range(1, ns):
            if k not in first:
                a2_wait(j, k)
                a3(j, k).start()

    for j in range(CHUNKS // 2):
        pass_on(j)
    for k in range(1, nx):
        for i in range(PIECES):
            for p in range(2):
                forward(k, i, p).wait_recv()
    lane = lax.broadcasted_iota(jnp.int32, m_s.shape[1:], 1)
    for g in range(1, ny):
        def later(k, carry, g=g):
            attend(g, xfrom(k))
            return carry

        lax.fori_loop(1, nx, later, 0)
        part_s[g - 1] = acc[g].astype(jnp.bfloat16)
        stat_s[g - 1] = jnp.where(lane == 0, m_s[g], l_s[g]).T[:stat_s.shape[1]]
        for copy in answer(g):
            copy.start()

    total = CORES * ns * nz * rows

    def project(j, sums):
        for k in range(ns):
            a3(j, k).wait_recv()
        for copy in weight_copies[j]:
            copy.wait()
        part = pl.ds(j * cw, cw)
        block = xs[:, :, :, part].reshape(total, cw)
        gate_j = jnp.dot(block, wg_v[part, :], preferred_element_type=jnp.float32)
        up_j = jnp.dot(block, wu_v[part, :], preferred_element_type=jnp.float32)
        return (gate_j, up_j) if sums is None else (sums[0] + gate_j, sums[1] + up_j)

    sums = None
    for j in range(CHUNKS):
        if j >= CHUNKS // 2:
            pass_on(j)
        if j >= 1:
            sums = project(j - 1, sums)
    gate_proj, up_proj = project(CHUNKS - 1, sums)
    gains = xs[:, :, :, width:].reshape(total, LANES).astype(jnp.float32)
    lane = lax.broadcasted_iota(jnp.int32, (total, LANES), 1)
    gain = jnp.sum(jnp.where((lane == e) | (lane == e + ne), gains, 0.0), axis=1, keepdims=True)
    hid[...] = (gate_proj / (1.0 + jnp.exp(-gate_proj)) * up_proj * gain).astype(jnp.bfloat16)

    def back1(j):
        return remote(pbuf.at[j, 1 - c], r1.at[j], b1_s.at[j], b1_r.at[j], sib)

    def back2(j, k):
        return remote(
            r2s.at[j, speer(k)], r2r.at[j, k - 1], b2_s.at[j, k - 1], b2_r.at[j, k - 1], (speer(k), e)
        )

    def back3(j, k):
        return remote(
            r3s.at[j, zpeer(k)], r3r.at[j, k - 1], b3_s.at[j, k - 1], b3_r.at[j, k - 1],
            (s, zpeer(k) * CORES + c),
        )

    def spread(j):
        back1(j).wait_recv()
        r2s[j] = (pbuf[j, c].astype(jnp.float32) + r1[j].astype(jnp.float32)).astype(jnp.bfloat16)
        for k in range(1, ns):
            back2(j, k).start()

    for j in range(CHUNKS):
        down_copies[j].wait()
        partial = jnp.dot(hid[...], wd_v[:, pl.ds(j * cw, cw)], preferred_element_type=jnp.float32)
        pbuf[j] = partial.astype(jnp.bfloat16).reshape(pbuf.shape[1:])
        back1(j).start()
        if j >= 1:
            spread(j - 1)
    spread(CHUNKS - 1)

    def last(k, carry):
        attend(0, xfrom(k))
        return carry

    lax.fori_loop(1, nx, last, 0)
    top, mass, value = m_s[0, :, :1], l_s[0, :, :1], acc[0]
    for k in range(1, ny):
        for copy in answer(k):
            copy.wait_recv()
        blank = jnp.zeros((LANES - stat_r.shape[1], stat_r.shape[2]), jnp.float32)
        stats = jnp.concatenate([stat_r[k - 1], blank], axis=0).T
        other = stats[:, :1]
        now = jnp.maximum(top, other)
        mine, theirs = jnp.exp(top - now), jnp.exp(other - now)
        mass = mass * mine + stats[:, 1:2] * theirs
        value = value * mine + part_r[k - 1].astype(jnp.float32) * theirs
        top = now
    attn_out[...] = (value / mass).astype(attn_out.dtype)
    attn_copy = pltpu.make_async_copy(attn_out, attn_hbm, io_sem.at[1])
    attn_copy.start()

    for j in range(CHUNKS):
        mine = r2s[j, s].astype(jnp.float32)
        for k in range(1, ns):
            back2(j, k).wait_recv()
            mine = mine + r2r[j, k - 1].astype(jnp.float32)
        asm[:, pl.ds(j * cw, cw)] = mine
        for i in range(nz):
            r3s[j, i] = asm[i * rows:(i + 1) * rows, pl.ds(j * cw, cw)].astype(jnp.bfloat16)
        for k in range(1, nz):
            back3(j, k).start()

    for j in range(CHUNKS):
        mine = r3s[j, z].astype(jnp.float32)
        for k in range(1, nz):
            back3(j, k).wait_recv()
            mine = mine + r3r[j, k - 1].astype(jnp.float32)
        moe_out[:, pl.ds(j * cw, cw)] = mine.astype(moe_out.dtype)

    for j in range(CHUNKS):
        for k in range(1, nz):
            a1(j, k).wait_send()
            back3(j, k).wait_send()
        for k in range(1, ns):
            a2_sent(j, k)
            back2(j, k).wait_send()
        for k in range(ns):
            a3(j, k).wait_send()
        back1(j).wait_send()
    for k in range(1, nx):
        for i in range(PIECES):
            share(k, i).wait_send()
            swap(k, i).wait_send()
            for p in range(2):
                forward(k, i, p).wait_send()
    attn_copy.wait()
    for k in range(1, ny):
        for copy in ask(k) + answer(k):
            copy.wait_send()


def hand_out(attn, moe, attn_out, moe_out):
    attn_out[...] = attn[...]
    moe_out[...] = moe[...]


def body(
    queries, own_latent, snapshots, leaf_snapshot, moe_input, expert_ids, gate_weights,
    w_gate, w_up, w_down,
):
    ns, ne = lax.axis_size("seq"), lax.axis_size("exp")
    rows, heads, kdim = queries.shape
    width, ff = moe_input.shape[1], w_gate.shape[2]
    nz = ne // CORES
    group = nz * rows
    snaps, positions = snapshots.shape[:2]
    nx = math.isqrt(ns)
    ny = ns // nx
    assert nx * ny == ns and ny > 1
    lines = rows * heads
    cw = width // CHUNKS
    bf16, f32 = jnp.bfloat16, jnp.float32
    vmem = pl.BlockSpec(memory_space=pltpu.VMEM)
    smem = pl.BlockSpec(memory_space=pltpu.SMEM)
    hbm = pl.BlockSpec(memory_space=pl.ANY)
    dma = pltpu.SemaphoreType.DMA
    attn, moe = pl.pallas_call(
        functools.partial(kernel, ns, ne),
        out_shape=(
            jax.ShapeDtypeStruct((rows * heads, LAT), bf16),
            jax.ShapeDtypeStruct((rows, width), bf16),
        ),
        in_specs=[hbm, vmem, hbm, smem, vmem, vmem, vmem, hbm, hbm, hbm],
        out_specs=(hbm, vmem),
        scratch_shapes=[
            pltpu.VMEM((width, ff), bf16),
            pltpu.VMEM((width, ff), bf16),
            pltpu.VMEM((ff, width), bf16),
            pltpu.VMEM((nx, snaps, kdim, positions), bf16),
            pltpu.VMEM((nz, rows, width + LANES), bf16),
            pltpu.VMEM((group, width + LANES), f32),
            pltpu.VMEM((CORES, ns, group, width + LANES), bf16),
            pltpu.VMEM((CORES * ns * group, ff), bf16),
            pltpu.VMEM((CHUNKS, CORES, ns, group, cw), bf16),
            pltpu.VMEM((CHUNKS, ns, group, cw), bf16),
            pltpu.VMEM((CHUNKS, ns, group, cw), bf16),
            pltpu.VMEM((CHUNKS, ns - 1, group, cw), bf16),
            pltpu.VMEM((CHUNKS, nz, rows, cw), bf16),
            pltpu.VMEM((CHUNKS, nz - 1, rows, cw), bf16),
            pltpu.VMEM((ny, lines, LANES), f32),
            pltpu.VMEM((ny, lines, LANES), f32),
            pltpu.VMEM((ny, lines, LAT), f32),
            pltpu.VMEM((lines, kdim), bf16),
            pltpu.VMEM((lines, LAT), bf16),
            pltpu.VMEM((ny - 1, lines, kdim), bf16),
            pltpu.VMEM((ny, 8, LANES), f32),
            pltpu.VMEM((ny - 1, lines, LAT), bf16),
            pltpu.VMEM((ny - 1, lines, LAT), bf16),
            pltpu.VMEM((ny - 1, 8, lines), f32),
            pltpu.VMEM((ny - 1, 8, lines), f32),
            dma((3, CHUNKS)),
            dma,
            dma((2,)),
            dma((CHUNKS, nz - 1)), dma((CHUNKS, nz - 1)),
            dma((CHUNKS, ns - 1)), dma((CHUNKS, ns - 1)),
            dma((CHUNKS, ns)), dma((CHUNKS, ns)),
            dma((nx - 1, PIECES)), dma((nx - 1, PIECES)),
            dma((nx - 1, PIECES)), dma((nx - 1, PIECES)),
            dma((nx - 1, PIECES, 2)), dma((nx - 1, PIECES, 2)),
            dma((CHUNKS,)), dma((CHUNKS,)),
            dma((CHUNKS, ns - 1)), dma((CHUNKS, ns - 1)),
            dma((CHUNKS, nz - 1)), dma((CHUNKS, nz - 1)),
            dma((ny - 1, 2)), dma((ny - 1, 2)),
            dma((ny - 1, 2)), dma((ny - 1, 2)),
        ],
        compiler_params=pltpu.CompilerParams(
            collective_id=0, has_side_effects=True, vmem_limit_bytes=62 * 1024 * 1024
        ),
    )(
        queries.reshape(rows * heads, kdim), own_latent, jnp.swapaxes(snapshots, 1, 2), leaf_snapshot,
        moe_input, expert_ids, gate_weights, w_gate, w_up, w_down,
    )
    attn, moe = pl.pallas_call(
        hand_out,
        out_shape=(jax.ShapeDtypeStruct(attn.shape, bf16), jax.ShapeDtypeStruct(moe.shape, bf16)),
        in_specs=[vmem, vmem],
        out_specs=(vmem, vmem),
    )(attn, moe)
    return attn.reshape(rows, heads, LAT), moe


def solution(mesh):
    in_specs = (
        P(("seq", "exp"), None, None),
        P(("seq", "exp"), None),
        P(None, "seq", None),
        P(("seq", "exp")),
        P(("seq", "exp"), None),
        P(("seq", "exp"), None),
        P(("seq", "exp"), None),
        P("exp", None, "seq"),
        P("exp", None, "seq"),
        P("exp", "seq", None),
    )
    out_specs = (P(("seq", "exp"), None, None), P(("seq", "exp"), None))
    return jax.shard_map(body, mesh=mesh, in_specs=in_specs, out_specs=out_specs, check_vma=False)
```
